128 devices in a mesh: dp: 8 (over y, core), expert: 16 (over x, z).
Axes of the slice: x: 4, y: 4, z: 4, core: 2. Of those that a mesh axis runs over, the one named last changes fastest.
Arguments:
- tokens: bfloat16 [16384, 2048], P(('dp', 'expert')), may hold values from -6 to 6
- expert_ids: int32 [16384, 8], P(('dp', 'expert')), may hold values from 0 to 15, all different within a row; in each aligned block of 128 rows (0 to 127, 128 to 255, ...) at most 68 rows name the same one
- gate_probs: bfloat16 [16384, 8], P(('dp', 'expert')), may hold values from 0.019897461 to 0.5
- out_grad: bfloat16 [16384, 2048], P(('dp', 'expert')), may hold values from -6 to 6
- w_gate: bfloat16 [16, 2048, 768], P('expert'), may hold values from -0.125 to 0.125
- w_up: bfloat16 [16, 2048, 768], P('expert'), may hold values from -0.125 to 0.125
- w_down: bfloat16 [16, 768, 2048], P('expert'), may hold values from -0.21875 to 0.21875
Outputs:
- token_grad: bfloat16 [16384, 2048], P(('dp', 'expert'))
- prob_grad: bfloat16 [16384, 8], P(('dp', 'expert'))
- gate_weight_grad: bfloat16 [16, 2048, 768], P('expert', 'dp')
- up_weight_grad: bfloat16 [16, 2048, 768], P('expert', 'dp')
- down_weight_grad: bfloat16 [16, 768, 2048], P('expert', None, 'dp')
The draws below stay inside these ranges and needn't reach their ends.
Inputs may be any that keep to these rules, and one draw needn't show every extreme that they name: `expert_ids`: each row names 8 different experts. Among the 128 rows of one device no expert is named more than 68 times, and in every draw some device names some expert exactly 68 times.
All inputs are finite; a program needn't handle non-finite values.
Results may differ from the reference program's by a relative error of at most 0.017.
Values may be sent and summed in bfloat16 or wider, within the bound.
No kernel may reach another device: no remote copies, remote signals or barrier semaphores. Data moves between devices by JAX's collectives and lax.ppermute only.
A program may use at most 128 MiB of HBM per device.

```python
import math
import jax
import jax.numpy as jnp
import numpy as np
from jax import lax

D = 2048
FF = 768
TOP = 8
TOK_DEV = 128
EXPERTS = 16
CAPACITY = 68
TOKENS = 16384
N_DP = 8
N_EXPERT = 16


def shard_levels(stream_key, extent, cuts, low, top_value):
    loudness, own = 1.0, jax.random.fold_in(stream_key, 6)
    for axis_at, shards_of in cuts:
        heights = jnp.exp(jax.random.uniform(jax.random.fold_in(own, axis_at), (shards_of,), jnp.float32, low / len(cuts), top_value / len(cuts)))
        loudness = loudness * jnp.repeat(heights, extent[axis_at] // shards_of).reshape([-1 if axis == axis_at else 1 for axis in range(len(extent))])
    return loudness


def routed_block(stream_key, own, number, rows, amount, top, limit, slope):
    sequence = jax.random.permutation(stream_key, amount)
    packed, usual = shares(amount, rows * top, limit, slope, True), shares(amount, rows * top, limit, slope, False)
    places = jnp.arange(amount)

    def named(lengths, rotation):
        used = int((lengths > 0).sum())
        fixed = max(1, used // 4)
        passed = fixed + (places - fixed + rotation * (used - fixed)) % max(1, amount - fixed)
        return jnp.zeros((amount,), jnp.int32).at[sequence[jnp.where(places < fixed, places, passed)]].set(jnp.asarray(lengths, jnp.int32))

    lengths = jnp.where(number % 4 == 0, named(packed, number // 4), named(usual, number - number // 4 - 1))
    mixed = jax.random.permutation(jax.random.fold_in(own, 3), amount)
    source_of, taker = mixed[0:amount // 2 * 2:2], mixed[1:amount // 2 * 2:2]
    slack = jnp.minimum(lengths[source_of] - 1, limit - lengths[taker]) // 2
    slack = jnp.where((source_of == sequence[0]) | (taker == sequence[0]) | (lengths[taker] == 0), 0, jnp.maximum(slack, 0))
    passed = jax.random.randint(jax.random.fold_in(own, 4), (amount // 2,), 0, 1 << 20) % (slack + 1)
    lengths = lengths.at[source_of].add(-passed).at[taker].add(passed)
    members = jnp.searchsorted(jnp.cumsum(lengths), jnp.arange(rows * top), side="right").astype(jnp.int32)
    listing = members.reshape(top, rows).T
    listing = listing[jax.random.permutation(jax.random.fold_in(own, 1), rows)]
    rotation = jax.random.randint(jax.random.fold_in(own, 2), (rows, 1), 0, top)
    return jnp.take_along_axis(listing, (jnp.arange(top)[None, :] + rotation) % top, axis=1)


def shares(amount, total, bound, skew, full):
    loads = [(1 << 20) // math.isqrt(standing ** skew) + 1 for standing in range(1, amount + 1)]
    largest = bound if full else min(bound, max(-(-total // amount), total * loads[0] // sum(loads)))
    least = 1 if total - largest >= amount - 1 else 0
    holding, spare = [largest] + [least] * (amount - 1), total - largest - least * (amount - 1)
    while spare > 0:
        movable = [i for i in range(1, amount) if holding[i] < largest] or [i for i in range(1, amount) if holding[i] < bound]
        pool, budget = sum([loads[i] for i in movable]), spare
        for i in movable:
            addition = min(bound - holding[i], max(1, budget * loads[i] // pool), spare)
            holding[i] = holding[i] + addition
            spare = spare - addition
    return np.array(holding)


def gaussian(rng, dims, spread, bound, pieces=(), kind=jnp.bfloat16):
    entries = spread * jax.random.normal(rng, dims, jnp.float32)
    if pieces:
        entries = entries * shard_levels(rng, dims, pieces, -0.22, 0.18)
    return jnp.clip(entries, -bound, bound).astype(kind)


def setup_inputs(seed: int = 0) -> dict:
    arg_keys = jax.random.split(jax.random.key(seed), 8)
    tokens = gaussian(arg_keys[0], (TOKENS, D), 1.0, 6.0, ((0, 128),))
    expert_ids_keys = jax.random.split(jax.random.fold_in(arg_keys[1], 1), TOKENS // TOK_DEV)
    expert_ids_turns = jax.random.permutation(jax.random.fold_in(arg_keys[1], 3), TOKENS // TOK_DEV)
    expert_ids = jax.vmap(lambda own, number: routed_block(jax.random.fold_in(arg_keys[1], 2), own, number, TOK_DEV, EXPERTS, TOP, CAPACITY, 2))(expert_ids_keys, expert_ids_turns).reshape((TOKENS, TOP))
    gate_probs = jnp.clip(jnp.exp(math.log(0.5) - 3.224016 * jax.random.uniform(arg_keys[2], (TOKENS, TOP), jnp.float32) ** shard_levels(arg_keys[2], (TOKENS, TOP), ((0, 128),), -0.2, 0.2)), 0.019897461, 0.5).astype(jnp.bfloat16)
    out_grad = gaussian(arg_keys[3], (TOKENS, D), 1.0, 6.0, ((0, 128),))
    w_gate = gaussian(arg_keys[4], (EXPERTS, D, FF), D ** -0.5, 0.125, ((0, 16),))
    w_up = gaussian(arg_keys[5], (EXPERTS, D, FF), D ** -0.5, 0.125, ((0, 16),))
    w_down = gaussian(arg_keys[6], (EXPERTS, FF, D), FF ** -0.5, 0.21875, ((0, 16),))
    return dict(tokens=tokens, expert_ids=expert_ids, gate_probs=gate_probs, out_grad=out_grad, w_gate=w_gate, w_up=w_up, w_down=w_down)


def expert_rows(rows_in, grad_in, weight_in, gate_mat, up_mat, down_mat):
    gate_pre = jnp.dot(rows_in, gate_mat, preferred_element_type=jnp.float32)
    up_pre = jnp.dot(rows_in, up_mat, preferred_element_type=jnp.float32)
    gate_sig = jax.nn.sigmoid(gate_pre)
    gate_act = gate_pre * gate_sig
    hidden = (gate_act * up_pre).astype(jnp.bfloat16)
    output = jnp.dot(hidden, down_mat, preferred_element_type=jnp.float32)
    grad_wide = grad_in.astype(jnp.float32)
    prob_part = jnp.sum(grad_wide * output, axis=1).astype(jnp.bfloat16)
    route_grad = (weight_in.astype(jnp.float32)[:, None] * grad_wide).astype(jnp.bfloat16)
    contract = (((1,), (1,)), ((), ()))
    hidden_grad = lax.dot_general(route_grad, down_mat, contract, preferred_element_type=jnp.float32)
    gate_back = (hidden_grad * up_pre * gate_sig * (1.0 + gate_pre * (1.0 - gate_sig))).astype(jnp.bfloat16)
    up_back = (hidden_grad * gate_act).astype(jnp.bfloat16)
    input_part = lax.dot_general(gate_back, gate_mat, contract, preferred_element_type=jnp.float32)
    input_part = (input_part + lax.dot_general(up_back, up_mat, contract, preferred_element_type=jnp.float32)).astype(jnp.bfloat16)
    return hidden, route_grad, gate_back, up_back, input_part, prob_part


def outer_sum(left, right):
    return lax.dot_general(left, right, (((0,), (0,)), ((), ())), preferred_element_type=jnp.float32)


def reference(tokens, expert_ids, gate_probs, out_grad, w_gate, w_up, w_down):
    per_group = TOK_DEV * N_EXPERT
    block_rows = math.gcd(per_group, 256)
    group_tokens = tokens.reshape(N_DP, per_group, D)
    group_ids = expert_ids.reshape(N_DP, per_group, TOP)
    group_probs = gate_probs.reshape(N_DP, per_group, TOP)
    group_grads = out_grad.reshape(N_DP, per_group, D)

    def one_group(totals, inputs):
        rows_g, ids_g, probs_g, grads_g = inputs

        def one_expert(state, expert):
            totals_in, input_acc, prob_acc = state
            hit = ids_g == expert
            routed = jnp.any(hit, axis=1)
            weight = jnp.sum(jnp.where(hit, probs_g.astype(jnp.float32), 0.0), axis=1).astype(jnp.bfloat16)
            order = jnp.argsort(jnp.where(routed, 0, 1).astype(jnp.int32), stable=True).astype(jnp.int32)
            live = jnp.sum(routed.astype(jnp.int32))
            gate_mat = w_gate[expert]
            up_mat = w_up[expert]
            down_mat = w_down[expert]

            def one_block(block_idx, carry):
                grad_gate, grad_up, grad_down, acc_in, acc_prob = carry
                picked = lax.dynamic_slice_in_dim(order, (block_idx * block_rows).astype(jnp.int32), block_rows)
                inside = (block_idx * block_rows + jnp.arange(block_rows, dtype=jnp.int32)) < live
                rows_in = rows_g[picked]
                block_weight = jnp.where(inside, weight[picked], jnp.zeros((), jnp.bfloat16))
                hidden, route_grad, gate_back, up_back, input_part, prob_part = expert_rows(
                    rows_in, grads_g[picked], block_weight, gate_mat, up_mat, down_mat)
                grad_gate = grad_gate + outer_sum(rows_in, gate_back)
                grad_up = grad_up + outer_sum(rows_in, up_back)
                grad_down = grad_down + outer_sum(hidden, route_grad)
                input_part = jnp.where(inside[:, None], input_part.astype(jnp.float32), 0.0)
                acc_in = acc_in.at[picked].add(input_part)
                prob_keep = jnp.where(hit[picked] & inside[:, None], prob_part.astype(jnp.float32)[:, None], 0.0)
                acc_prob = acc_prob.at[picked].add(prob_keep)
                return grad_gate, grad_up, grad_down, acc_in, acc_prob

            start_state = (jnp.zeros((D, FF), jnp.float32), jnp.zeros((D, FF), jnp.float32),
                           jnp.zeros((FF, D), jnp.float32), input_acc, prob_acc)
            block_total = (live + block_rows - 1) // block_rows
            grad_gate, grad_up, grad_down, input_acc, prob_acc = lax.fori_loop(0, block_total, one_block, start_state)
            total_gate, total_up, total_down = totals_in
            total_gate = total_gate.at[expert].add(lax.optimization_barrier(grad_gate.astype(jnp.bfloat16)).astype(jnp.float32))
            total_up = total_up.at[expert].add(lax.optimization_barrier(grad_up.astype(jnp.bfloat16)).astype(jnp.float32))
            total_down = total_down.at[expert].add(lax.optimization_barrier(grad_down.astype(jnp.bfloat16)).astype(jnp.float32))
            return ((total_gate, total_up, total_down), input_acc, prob_acc), None

        start_inner = (totals, jnp.zeros((per_group, D), jnp.float32), jnp.zeros((per_group, TOP), jnp.float32))
        (totals, input_acc, prob_acc), unused = lax.scan(one_expert, start_inner, jnp.arange(EXPERTS, dtype=jnp.int32))
        return totals, (input_acc, prob_acc)

    start_totals = (jnp.zeros((EXPERTS, D, FF), jnp.float32), jnp.zeros((EXPERTS, D, FF), jnp.float32),
                    jnp.zeros((EXPERTS, FF, D), jnp.float32))
    totals, (input_all, prob_all) = lax.scan(one_group, start_totals, (group_tokens, group_ids, group_probs, group_grads))
    token_grad = input_all.reshape(TOKENS, D).astype(jnp.bfloat16)
    prob_grad = prob_all.reshape(TOKENS, TOP).astype(jnp.bfloat16)
    return (token_grad, prob_grad, totals[0].astype(jnp.bfloat16), totals[1].astype(jnp.bfloat16),
            totals[2].astype(jnp.bfloat16))
```

```python
import jax
import jax.numpy as jnp
from jax import lax
from jax.sharding import PartitionSpec as P

AXES = ("dp", "expert")
SIDE = 4
BF = jnp.bfloat16
F32 = jnp.float32


def coords(expert):
    return expert // SIDE, expert % SIDE


def shifted(value, step, first, n_dp):
    pairs = []
    for dp in range(n_dp):
        along_x = first == (dp % 2 == 0)
        for e in range(SIDE * SIDE):
            x, z = coords(e)
            if along_x:
                to = ((x + step) % SIDE) * SIDE + z
            else:
                to = x * SIDE + (z + step) % SIDE
            pairs.append((dp * SIDE * SIDE + e, dp * SIDE * SIDE + to))
    return lax.ppermute(value, AXES, pairs)


def outer_sum(left, right):
    return lax.dot_general(left, right, (((0,), (0,)), ((), ())), preferred_element_type=F32)


def body(tokens, expert_ids, gate_probs, out_grad, w_gate, w_up, w_down):
    rows_dev, width = tokens.shape
    fanout = expert_ids.shape[1]
    n_dp = lax.axis_size("dp")
    groups = lax.axis_size("expert")
    mean_load = rows_dev * fanout // groups
    capacity = min(rows_dev, mean_load + max(2, rows_dev * fanout // (16 * groups)))
    block = SIDE * capacity
    group_rows = SIDE * rows_dev

    dp_at = lax.axis_index("dp")
    e_at = lax.axis_index("expert")
    x_at, z_at = coords(e_at)
    even = dp_at % 2 == 0
    a_at = jnp.where(even, x_at, z_at)
    b_at = jnp.where(even, z_at, x_at)

    def expert_of(a, b):
        a, b = a % SIDE, b % SIDE
        return jnp.where(even, a * SIDE + b, b * SIDE + a)

    send = lambda v, step, first: v if step == 0 else shifted(v, step, first, n_dp)

    meta = jnp.concatenate([expert_ids.astype(BF).T, gate_probs.T], axis=0)
    metas = [send(meta, s, True) for s in range(SIDE)]
    toks = [send(tokens, s, True) for s in range(SIDE)]
    grds = [send(out_grad, s, True) for s in range(SIDE)]

    ids_g = jnp.concatenate([m[:fanout] for m in metas], axis=1).astype(jnp.int32)
    pr_g = jnp.concatenate([m[fanout:] for m in metas], axis=1).astype(F32)
    dests = jnp.stack([expert_of(a_at, b_at + d) for d in range(SIDE)]).astype(jnp.int32)
    hit_k = ids_g[None] == dests[:, None, None]
    hit = jnp.any(hit_k, axis=1)
    prob = jnp.sum(jnp.where(hit_k, pr_g[None], 0.0), axis=1)
    order = jnp.arange(group_rows, dtype=jnp.int32)
    tri = (order[:, None] < order[None, :]).astype(BF)
    rank = jnp.dot(hit.astype(BF), tri, preferred_element_type=F32).astype(jnp.int32)
    rank = jnp.where(hit, rank, -1)
    slots = jnp.arange(block, dtype=jnp.int32)
    pick = (rank[:, None, :] == slots[None, :, None])
    picker = pick.astype(BF).reshape(SIDE * block, group_rows)
    weigher = jnp.where(pick, prob[:, None, :], 0.0).astype(BF).reshape(SIDE * block, group_rows)

    tok_rows = jnp.dot(picker, jnp.concatenate(toks, 0), preferred_element_type=F32).astype(BF)
    grd_rows = jnp.dot(weigher, jnp.concatenate(grds, 0), preferred_element_type=F32).astype(BF)
    cut = lambda v, d: v[d * block : (d + 1) * block]
    rows_in = jnp.concatenate([send(cut(tok_rows, d), d, False) for d in range(SIDE)], 0)
    route_grad = jnp.concatenate([send(cut(grd_rows, d), d, False) for d in range(SIDE)], 0)

    gate_mat, up_mat, down_mat = w_gate[0], w_up[0], w_down[0]
    contract = (((1,), (1,)), ((), ()))
    gate_pre = jnp.dot(rows_in, gate_mat, preferred_element_type=F32)
    up_pre = jnp.dot(rows_in, up_mat, preferred_element_type=F32)
    gate_sig = jax.nn.sigmoid(gate_pre)
    gate_act = gate_pre * gate_sig
    hidden = (gate_act * up_pre).astype(BF)
    hidden_grad = lax.dot_general(route_grad, down_mat, contract, preferred_element_type=F32)
    dots = jnp.sum(hidden.astype(F32) * hidden_grad, axis=1)
    gate_back = (hidden_grad * up_pre * gate_sig * (1.0 + gate_pre * (1.0 - gate_sig))).astype(BF)
    up_back = (hidden_grad * gate_act).astype(BF)
    input_part = lax.dot_general(gate_back, gate_mat, contract, preferred_element_type=F32)
    input_part = (
        input_part + lax.dot_general(up_back, up_mat, contract, preferred_element_type=F32)
    ).astype(BF)

    own_block = jnp.arange(SIDE * block, dtype=jnp.int32) // block
    dot_cols = jnp.where(own_block[:, None] == jnp.arange(SIDE)[None, :], dots[:, None], 0.0).astype(BF)
    back = jnp.concatenate([send(cut(input_part, d), -d, False) for d in range(SIDE)], 0)
    back_dots = jnp.concatenate([send(cut(dot_cols, d), -d, False) for d in range(SIDE)], 0)
    part = outer_sum(picker, back).astype(BF)
    part_dots = outer_sum(picker, back_dots).astype(BF)
    piece = lambda v, s: v[s * rows_dev : (s + 1) * rows_dev]
    token_grad = sum(send(piece(part, s), -s, True).astype(F32) for s in range(SIDE)).astype(BF)
    prob_grad = jnp.zeros(expert_ids.shape, F32)
    for s in range(SIDE):
        vals = send(piece(part_dots, s), -s, True).astype(F32)
        for d in range(SIDE):
            prob_grad += jnp.where(expert_ids == expert_of(a_at + s, b_at + d), vals[:, d : d + 1], 0.0)
    prob_grad = (prob_grad / gate_probs.astype(F32)).astype(BF)

    terms = jnp.concatenate(
        [
            outer_sum(rows_in, gate_back).astype(BF),
            outer_sum(rows_in, up_back).astype(BF),
            outer_sum(route_grad, hidden).astype(BF),
        ],
        axis=1,
    )
    ff = gate_mat.shape[1]
    owned = lax.psum_scatter(terms, "dp", scatter_dimension=0, tiled=True)
    return (
        token_grad,
        prob_grad,
        owned[:, :ff][None],
        owned[:, ff : 2 * ff][None],
        jnp.transpose(owned[:, 2 * ff :])[None],
    )


def solution(mesh):
    rows = P(("dp", "expert"), None)
    mats = P("expert", None, None)
    return jax.shard_map(
        body,
        mesh=mesh,
        in_specs=(rows, rows, rows, rows, mats, mats, mats),
        out_specs=(rows, rows, P("expert", "dp", None), P("expert", "dp", None), P("expert", None, "dp")),
        check_vma=False,
    )
```

```python
import jax
import jax.numpy as jnp
from jax import lax
from jax.experimental import pallas as pl
from jax.experimental.pallas import tpu as pltpu
from jax.sharding import PartitionSpec as P

AXES = ("dp", "expert")
SIDE = 4
BF = jnp.bfloat16
F32 = jnp.float32
TILE = 256
VMEM_LIMIT = 40 * 2**20

ANY = pl.BlockSpec(memory_space=pl.ANY)
NT = (((1,), (1,)), ((), ()))
TN = (((0,), (0,)), ((), ()))


def coords(expert):
    return expert // SIDE, expert % SIDE


def permuted(value, n_dp, target):
    pairs = []
    for dp in range(n_dp):
        for e in range(SIDE * SIDE):
            y, c, x, z = target(dp // 2, dp % 2, *coords(e))
            to = (y % SIDE * 2 + c) * SIDE * SIDE + x % SIDE * SIDE + z % SIDE
            pairs.append((dp * SIDE * SIDE + e, to))
    return lax.ppermute(value, AXES, pairs)


def call(kernel, grid, in_specs, out_specs, out_shape, args, scratch=(), flops=0, after=(), prefetch=()):
    n_after, n_pre, n_in = len(after), len(prefetch), len(args)

    def run(*refs):
        kernel(*refs[:n_pre], *refs[n_pre + n_after :])

    bytes_moved = sum(a.size * a.dtype.itemsize for a in args)
    bytes_moved += sum(s.size * jnp.dtype(s.dtype).itemsize for s in out_shape)
    return pl.pallas_call(
        run,
        grid_spec=pltpu.PrefetchScalarGridSpec(
            num_scalar_prefetch=n_pre,
            grid=grid,
            in_specs=[ANY] * n_after + list(in_specs),
            out_specs=list(out_specs),
            scratch_shapes=list(scratch),
        ),
        out_shape=list(out_shape),
        compiler_params=pltpu.CompilerParams(vmem_limit_bytes=VMEM_LIMIT),
        cost_estimate=pl.CostEstimate(flops=flops, bytes_accessed=bytes_moved, transcendentals=0),
    )(*prefetch, *after, *args)


def gather_blocks(blocks, whole, sems):
    rows = whole.shape[0] // len(blocks)
    copies = [
        pltpu.make_async_copy(b, whole.at[pl.ds(i * rows, rows), :], sems.at[i]) for i, b in enumerate(blocks)
    ]
    for c in copies:
        c.start()
    for c in copies:
        c.wait()


def shape(dims, kind=BF):
    return jax.ShapeDtypeStruct(dims, kind)


def pick_rows(picker, sources, block):
    group, width = picker.shape[1], sources[0].shape[1]

    def kernel(pick, x0, x1, x2, x3, o0, o1, o2, o3, whole, sems):
        gather_blocks((x0, x1, x2, x3), whole, sems)
        for at in range(0, width, 512):
            for d, o in enumerate((o0, o1, o2, o3)):
                o[:, at : at + 512] = jnp.dot(
                    pick[d * block : (d + 1) * block, :],
                    whole[:, at : at + 512],
                    preferred_element_type=F32,
                ).astype(BF)

    full = lambda r, c: pl.BlockSpec((r, c), lambda i: (0, 0))
    return call(
        kernel,
        (1,),
        [full(*picker.shape)] + [ANY] * SIDE,
        [full(block, width)] * SIDE,
        [shape((block, width))] * SIDE,
        [picker, *sources],
        [pltpu.VMEM((group, width), BF), pltpu.SemaphoreType.DMA((SIDE,))],
        2 * picker.size * width,
    )


def forward(blocks, gate_mat, up_mat):
    block, width = blocks[0].shape
    ff = gate_mat.shape[1]
    rows = SIDE * block
    half = rows // 2

    def kernel(x0, x1, x2, x3, wg, wu, gate_k, up_k, hidden, whole, sems):
        @pl.when(pl.program_id(0) == 0)
        def _():
            gather_blocks((x0, x1, x2, x3), whole, sems)

        for h in (0, half):
            x = whole[h : h + half, :]
            g = jnp.dot(x, wg[...], preferred_element_type=F32)
            u = jnp.dot(x, wu[...], preferred_element_type=F32)
            s = jax.nn.sigmoid(g)
            act = g * s
            hidden[h : h + half, :] = (act * u).astype(BF)
            gate_k[h : h + half, :] = u * s * (1.0 + g * (1.0 - s))
            up_k[h : h + half, :] = act

    col = lambda r: pl.BlockSpec((r, TILE), lambda j: (0, j))
    return call(
        kernel,
        (ff // TILE,),
        [ANY] * SIDE + [col(width)] * 2,
        [col(rows)] * 3,
        [shape((rows, ff), F32), shape((rows, ff), F32), shape((rows, ff))],
        [*blocks, gate_mat, up_mat],
        [pltpu.VMEM((rows, width), BF), pltpu.SemaphoreType.DMA((SIDE,))],
        4 * rows * width * ff,
    )


def back_hidden(blocks, down_mat, gate_k, up_k, hidden, after=()):
    block, width = blocks[0].shape
    ff = down_mat.shape[0]
    rows = SIDE * block
    half = rows // 2

    def kernel(x0, x1, x2, x3, wd, gk, uk, hid, gate_back, up_back, dots, whole, total, sems):
        j = pl.program_id(0)

        @pl.when(j == 0)
        def _():
            gather_blocks((x0, x1, x2, x3), whole, sems)
            total[...] = jnp.zeros_like(total)

        for h in (0, half):
            at = slice(h, h + half)
            hg = lax.dot_general(whole[at, :], wd[...], NT, preferred_element_type=F32)
            gate_back[at, :] = (hg * gk[at, :]).astype(BF)
            up_back[at, :] = (hg * uk[at, :]).astype(BF)
            total[at, :] += jnp.sum(hg * hid[at, :].astype(F32), axis=1, keepdims=True)

        @pl.when(j == pl.num_programs(0) - 1)
        def _():
            for d in range(SIDE):
                at = slice(d * block, (d + 1) * block)
                lane = lax.broadcasted_iota(jnp.int32, (block, 128), 1)
                dots[at, :] = jnp.where(lane == d, total[at, :], 0.0).astype(BF)

    col = pl.BlockSpec((rows, TILE), lambda j: (0, j))
    return call(
        kernel,
        (ff // TILE,),
        [ANY] * SIDE + [pl.BlockSpec((TILE, width), lambda j: (j, 0)), col, col, col],
        [col, col, pl.BlockSpec((rows, 128), lambda j: (0, 0))],
        [shape((rows, ff)), shape((rows, ff)), shape((rows, 128))],
        [*blocks, down_mat, gate_k, up_k, hidden],
        [pltpu.VMEM((rows, width), BF), pltpu.VMEM((rows, 1), F32), pltpu.SemaphoreType.DMA((SIDE,))],
        2 * rows * width * ff,
        after,
    )


def back_input(gate_back, up_back, gate_mat, up_mat, first, count, dots, after=()):
    rows, ff = gate_back.shape
    block = rows // SIDE
    extra = 0 if dots is None else dots.shape[1]

    def kernel(gb, ub, wg, wu, *refs):
        outs = refs[-SIDE:]
        n = pl.program_id(0)
        val = lax.dot_general(gb[...], wg[...], NT, preferred_element_type=F32)
        val += lax.dot_general(ub[...], wu[...], NT, preferred_element_type=F32)
        val = val.astype(BF)
        for d, o in enumerate(outs):
            o[:, pl.ds(pl.multiple_of(n * TILE, TILE), TILE)] = val[d * block : (d + 1) * block, :]
        if extra:

            @pl.when(n == 0)
            def _():
                for d, o in enumerate(outs):
                    o[:, count : count + extra] = refs[0][d * block : (d + 1) * block, :]

    full = lambda r, c: pl.BlockSpec((r, c), lambda n: (0, 0))
    weight = pl.BlockSpec((TILE, ff), lambda n: (first // TILE + n, 0))
    return call(
        kernel,
        (count // TILE,),
        [full(rows, ff)] * 2 + [weight] * 2 + [full(rows, extra)] * (extra > 0),
        [full(block, count + extra)] * SIDE,
        [shape((block, count + extra))] * SIDE,
        [gate_back, up_back, gate_mat, up_mat] + [dots] * (extra > 0),
        (),
        4 * rows * count * ff,
        after,
    )


def weight_terms(blocks, others, order, after=()):
    block, width = blocks[0].shape
    rows = SIDE * block
    ff = others[0].shape[1]
    n = len(others)

    def kernel(order_ref, x0, x1, x2, x3, *refs):
        out, tall = refs[n], refs[n + 1]
        for d, x in enumerate((x0, x1, x2, x3)):
            tall[d * block : (d + 1) * block, :] = x[...]
        for i in range(n):
            out[0, i * TILE : (i + 1) * TILE, :] = lax.dot_general(
                tall[...], refs[i][...], TN, preferred_element_type=F32
            ).astype(BF)

    return call(
        kernel,
        (SIDE,),
        [pl.BlockSpec((block, TILE), lambda k, o: (0, o[k]))] * SIDE
        + [pl.BlockSpec((rows, ff), lambda k, o: (0, 0))] * n,
        [pl.BlockSpec((1, n * TILE, ff), lambda k, o: (k, 0, 0))],
        [shape((SIDE, n * TILE, ff))],
        [*blocks, *others],
        [pltpu.VMEM((rows, TILE), BF)],
        2 * n * rows * SIDE * TILE * ff,
        after,
        [order],
    )[0]


def merge_rows(placer, blocks, after=()):
    group = placer.shape[0]
    block, width = blocks[0].shape
    rows_dev = group // SIDE

    def kernel(place, x0, x1, x2, x3, o0, o1, o2, o3, whole, sems):
        gather_blocks((x0, x1, x2, x3), whole, sems)
        for at in range(0, width, TILE):
            cols = slice(at, min(at + TILE, width))
            val = jnp.dot(place[...], whole[:, cols], preferred_element_type=F32).astype(BF)
            for s, o in enumerate((o0, o1, o2, o3)):
                o[:, cols] = val[s * rows_dev : (s + 1) * rows_dev, :]

    full = lambda r, c: pl.BlockSpec((r, c), lambda i: (0, 0))
    return call(
        kernel,
        (1,),
        [full(*placer.shape)] + [ANY] * SIDE,
        [full(rows_dev, width)] * SIDE,
        [shape((rows_dev, width))] * SIDE,
        [placer, *blocks],
        [pltpu.VMEM((SIDE * block, width), BF), pltpu.SemaphoreType.DMA((SIDE,))],
        2 * placer.size * width,
        after,
    )


def plus(*terms):
    return sum(t.astype(F32) for t in terms).astype(BF)


def body(tokens, expert_ids, gate_probs, out_grad, w_gate, w_up, w_down):
    rows_dev, width = tokens.shape
    fanout = expert_ids.shape[1]
    n_dp = lax.axis_size("dp")
    groups = lax.axis_size("expert")
    mean_load = rows_dev * fanout // groups
    capacity = min(rows_dev, mean_load + max(2, rows_dev * fanout // (16 * groups)))
    block = SIDE * capacity
    group_rows = SIDE * rows_dev

    dp_at = lax.axis_index("dp")
    x_at, z_at = coords(lax.axis_index("expert"))
    even = dp_at % 2 == 0
    a_at = jnp.where(even, x_at, z_at)
    b_at = jnp.where(even, z_at, x_at)

    def expert_of(a, b):
        a, b = a % SIDE, b % SIDE
        return jnp.where(even, a * SIDE + b, b * SIDE + a)

    def along(v, step, core):
        if step % SIDE == 0:
            return v
        return permuted(
            v, n_dp, lambda y, c, x, z: (y, c, x + step, z) if c == core else (y, c, x, z + step)
        )

    first = lambda v, step: along(v, step, 0)
    second = lambda v, step: along(v, step, 1)
    swap = lambda v: permuted(v, n_dp, lambda y, c, x, z: (y, 1 - c, x, z))
    up_y = lambda v, step: permuted(v, n_dp, lambda y, c, x, z: (y + step, c, x, z))

    toks = [first(tokens, s) for s in range(SIDE)]
    meta = jnp.concatenate([expert_ids.astype(BF).T, gate_probs.T], axis=0)
    metas = [first(meta, s) for s in range(SIDE)]
    grds = [first(out_grad, s) for s in range(SIDE)]

    ids_g = jnp.concatenate([m[:fanout] for m in metas], axis=1).astype(jnp.int32)
    pr_g = jnp.concatenate([m[fanout:] for m in metas], axis=1).astype(F32)
    dests = jnp.stack([expert_of(a_at, b_at + d) for d in range(SIDE)]).astype(jnp.int32)
    hit_k = ids_g[None] == dests[:, None, None]
    hit = jnp.any(hit_k, axis=1)
    prob = jnp.sum(jnp.where(hit_k, pr_g[None], 0.0), axis=1)
    order = jnp.arange(group_rows, dtype=jnp.int32)
    tri = (order[:, None] < order[None, :]).astype(BF)
    rank = jnp.dot(hit.astype(BF), tri, preferred_element_type=F32).astype(jnp.int32)
    rank = jnp.where(hit, rank, -1)
    slots = jnp.arange(block, dtype=jnp.int32)
    pick = rank[:, None, :] == slots[None, :, None]
    picker = pick.astype(BF).reshape(SIDE * block, group_rows)
    weigher = jnp.where(pick, prob[:, None, :], 0.0).astype(BF).reshape(SIDE * block, group_rows)
    placer = picker.T

    rows_in = [second(v, d) for d, v in enumerate(pick_rows(picker, toks, block))]
    route_grad = [second(v, d) for d, v in enumerate(pick_rows(weigher, grds, block))]

    gate_mat, up_mat, down_mat = w_gate[0], w_up[0], w_down[0]
    gate_k, up_k, hidden = forward(rows_in, gate_mat, up_mat)

    y_at, c_at = dp_at // 2, dp_at % 2
    near = (y_at + jnp.arange(SIDE, dtype=jnp.int32)) % SIDE * 2
    keep_order, give_order = near + c_at, near + 1 - c_at

    give_down = weight_terms(route_grad, [hidden], give_order)
    gate_back, up_back, dots = back_hidden(route_grad, down_mat, gate_k, up_k, hidden, [give_down])
    cut = width // 2
    in_0 = back_input(gate_back, up_back, gate_mat, up_mat, 0, cut, dots)
    keep_down = weight_terms(route_grad, [hidden], keep_order, [in_0[0]])
    give_gu = weight_terms(rows_in, [gate_back, up_back], give_order, [keep_down])
    in_1 = back_input(gate_back, up_back, gate_mat, up_mat, cut, width - cut, None, [give_gu])
    keep_gu = weight_terms(rows_in, [gate_back, up_back], keep_order, [in_1[0]])

    def over_dp(keep, give):
        got = swap(give)
        acc = [plus(keep[k], got[k]) for k in range(SIDE)]
        h = keep.shape[1] // 2
        far_up = up_y(acc[2][:h], 1)
        far_down = up_y(acc[2][h:], -1)
        up_hi = up_y(acc[1][h:], 1)
        down_lo = up_y(acc[3][:h], -1)
        up_lo = up_y(plus(acc[1][:h], far_up), 1)
        down_hi = up_y(plus(acc[3][h:], far_down), -1)
        return jnp.concatenate(
            [plus(acc[0][:h], up_lo, down_lo), plus(acc[0][h:], up_hi, down_hi)], axis=0
        )

    down_own = over_dp(keep_down, give_down)
    gu_own = over_dp(keep_gu, give_gu)

    sums = []
    for part in (in_0, in_1):
        back = [second(v, -d) for d, v in enumerate(part)]
        merged = merge_rows(placer, back)
        sums.append([first(v, -s) for s, v in enumerate(merged)])
    token_grad = jnp.concatenate([plus(*[v[:, :cut] for v in sums[0]]), plus(*sums[1])], axis=1)
    prob_grad = jnp.zeros(expert_ids.shape, F32)
    for s in range(SIDE):
        vals = sums[0][s][:, cut:].astype(F32)
        for d in range(SIDE):
            prob_grad += jnp.where(expert_ids == expert_of(a_at + s, b_at + d), vals[:, d : d + 1], 0.0)
    prob_grad = (prob_grad / gate_probs.astype(F32)).astype(BF)

    return (
        token_grad,
        prob_grad,
        gu_own[:TILE][None],
        gu_own[TILE:][None],
        jnp.transpose(down_own)[None],
    )


def solution(mesh):
    rows = P(("dp", "expert"), None)
    mats = P("expert", None, None)
    return jax.shard_map(
        body,
        mesh=mesh,
        in_specs=(rows, rows, rows, rows, mats, mats, mats),
        out_specs=(rows, rows, P("expert", "dp", None), P("expert", "dp", None), P("expert", None, "dp")),
        check_vma=False,
    )
```

```python
import jax
import jax.numpy as jnp
from jax import lax
from jax.experimental import pallas as pl
from jax.experimental.pallas import tpu as pltpu
from jax.sharding import PartitionSpec as P

AXES = ("dp", "expert")
SIDE = 4
BF = jnp.bfloat16
F32 = jnp.float32
TILE = 256
VMEM_LIMIT = 60 * 2**20

ANY = pl.BlockSpec(memory_space=pl.ANY)
NT = (((1,), (1,)), ((), ()))
TN = (((0,), (0,)), ((), ()))


def coords(expert):
    return expert // SIDE, expert % SIDE


def permuted(value, n_dp, target):
    pairs = []
    for dp in range(n_dp):
        for e in range(SIDE * SIDE):
            y, c, x, z = target(dp // 2, dp % 2, *coords(e))
            to = (y % SIDE * 2 + c) * SIDE * SIDE + x % SIDE * SIDE + z % SIDE
            pairs.append((dp * SIDE * SIDE + e, to))
    return lax.ppermute(value, AXES, pairs)


def call(kernel, grid, in_specs, out_specs, out_shape, args, scratch=(), after=(), prefetch=()):
    n_after, n_pre = len(after), len(prefetch)

    def run(*refs):
        kernel(*refs[:n_pre], *refs[n_pre + n_after :])

    return pl.pallas_call(
        run,
        grid_spec=pltpu.PrefetchScalarGridSpec(
            num_scalar_prefetch=n_pre,
            grid=grid,
            in_specs=[ANY] * n_after + list(in_specs),
            out_specs=list(out_specs),
            scratch_shapes=list(scratch),
        ),
        out_shape=list(out_shape),
        compiler_params=pltpu.CompilerParams(vmem_limit_bytes=VMEM_LIMIT),
        cost_estimate=pl.CostEstimate(flops=1000, bytes_accessed=1000, transcendentals=0),
    )(*prefetch, *after, *args)


def block_copies(blocks, whole, sems, col=0):
    rows, width = whole.shape[0] // len(blocks), whole.shape[1]
    return [
        pltpu.make_async_copy(b.at[:, pl.ds(col, width)], whole.at[pl.ds(i * rows, rows), :], sems.at[i])
        for i, b in enumerate(blocks)
    ]


def gather_blocks(blocks, whole, sems, col=0):
    copies = block_copies(blocks, whole, sems, col)
    for c in copies:
        c.start()
    for c in copies:
        c.wait()


def shape(dims, kind=BF):
    return jax.ShapeDtypeStruct(dims, kind)


def onehot_dots(onehot, whole, outs, block):
    width = whole.shape[1]
    for d, o in enumerate(outs):
        hot = onehot(d)
        for at in range(0, width, 512):
            cols = slice(at, at + 512)
            o[:, cols] = jnp.dot(hot, whole[:, cols], preferred_element_type=F32).astype(BF)


def pick_tokens(sources, dests, width, fanout, block):
    rows_dev = sources[0].shape[0]
    group = SIDE * rows_dev

    def kernel(dest, x0, x1, x2, x3, o0, o1, o2, o3, slot, weight, whole, meta, sems, meta_sems):
        metas = block_copies((x0, x1, x2, x3), meta, meta_sems, 2 * width)
        copies = block_copies((x0, x1, x2, x3), whole, sems)
        for c in metas + copies:
            c.start()
        for c in metas:
            c.wait()
        hits, probs = [], []
        sheets = [jnp.transpose(meta[s * rows_dev : (s + 1) * rows_dev, :].astype(F32)) for s in range(SIDE)]
        for d in range(SIDE):
            hit, prob = [], []
            for m in sheets:
                same = jnp.where(m[:fanout, :] == dest[d].astype(F32), 1.0, 0.0)
                hit.append(jnp.sum(same, axis=0, keepdims=True))
                prob.append(jnp.sum(same * m[fanout : 2 * fanout, :], axis=0, keepdims=True))
            hits.append(jnp.concatenate(hit, axis=1))
            probs.append(jnp.concatenate(prob, axis=1))
        hits = jnp.concatenate(hits + [jnp.zeros((SIDE, group), F32)], axis=0)
        probs = jnp.concatenate(probs + [jnp.zeros((SIDE, group), F32)], axis=0)
        earlier = lax.broadcasted_iota(jnp.int32, (group, group), 0) < lax.broadcasted_iota(
            jnp.int32, (group, group), 1
        )
        rank = jnp.dot(
            hits.astype(BF), jnp.where(earlier, 1.0, 0.0).astype(BF), preferred_element_type=F32
        )
        slot[...] = jnp.where(hits > 0.5, rank, -4096.0)
        weight[...] = probs
        for c in copies:
            c.wait()
        row = lax.broadcasted_iota(jnp.int32, (block, group), 0).astype(F32)
        onehot_dots(
            lambda d: jnp.where(row == slot[d : d + 1, :], 1.0, 0.0).astype(BF), whole, (o0, o1, o2, o3), block
        )

    full = lambda r, c: pl.BlockSpec((r, c), lambda i, o: (0, 0))
    return call(
        kernel,
        (1,),
        [ANY] * SIDE,
        [full(block, width)] * SIDE + [full(2 * SIDE, group)] * 2,
        [shape((block, width))] * SIDE + [shape((2 * SIDE, group), F32)] * 2,
        sources,
        [
            pltpu.VMEM((group, width), BF),
            pltpu.VMEM((group, 128), BF),
            pltpu.SemaphoreType.DMA((SIDE,)),
            pltpu.SemaphoreType.DMA((SIDE,)),
        ],
        prefetch=[dests],
    )


def pick_grads(sources, slot, weight, width, block, after):
    rows_dev = sources[0].shape[0]
    group = SIDE * rows_dev

    def kernel(slot, weight, x0, x1, x2, x3, o0, o1, o2, o3, place, whole, sems):
        copies = block_copies((x0, x1, x2, x3), whole, sems, width)
        for c in copies:
            c.start()
        tall = jnp.transpose(jnp.concatenate([slot[...]] * 16, axis=0))
        lane = lax.broadcasted_iota(jnp.int32, (group, SIDE * block), 1).astype(F32)
        back = jnp.zeros((group, SIDE * block), F32)
        for d in range(SIDE):
            back = jnp.where(lane == tall[:, d : d + 1] + float(d * block), 1.0, back)
        place[...] = back.astype(BF)
        for c in copies:
            c.wait()
        row = lax.broadcasted_iota(jnp.int32, (block, group), 0).astype(F32)
        onehot_dots(
            lambda d: jnp.where(row == slot[d : d + 1, :], weight[d : d + 1, :], 0.0).astype(BF),
            whole,
            (o0, o1, o2, o3),
            block,
        )

    full = lambda r, c: pl.BlockSpec((r, c), lambda i: (0, 0))
    return call(
        kernel,
        (1,),
        [full(2 * SIDE, group)] * 2 + [ANY] * SIDE,
        [full(block, width)] * SIDE + [full(group, SIDE * block)],
        [shape((block, width))] * SIDE + [shape((group, SIDE * block))],
        [slot, weight, *sources],
        [pltpu.VMEM((group, width), BF), pltpu.SemaphoreType.DMA((SIDE,))],
        after=after,
    )


def forward(blocks, gate_mat, up_mat, after):
    block, width = blocks[0].shape
    ff = gate_mat.shape[1]
    rows = SIDE * block
    half = rows // 2
    steps = ff // TILE

    def kernel(x0, x1, x2, x3, wg, wu, gate_k, up_k, hidden, hidden_t, whole, sems):
        @pl.when(pl.program_id(0) == 0)
        def _():
            gather_blocks((x0, x1, x2, x3), whole, sems)

        for h in (0, half):
            x = whole[h : h + half, :]
            g = jnp.dot(x, wg[...], preferred_element_type=F32)
            u = jnp.dot(x, wu[...], preferred_element_type=F32)
            s = jax.nn.sigmoid(g)
            act = g * s
            hidden[h : h + half, :] = (act * u).astype(BF)
            gate_k[h : h + half, :] = u * s * (1.0 + g * (1.0 - s))
            up_k[h : h + half, :] = act
        hidden_t[...] = jnp.transpose(hidden[...])

    col = lambda r: pl.BlockSpec((r, TILE), lambda j: (0, j))
    return call(
        kernel,
        (steps,),
        [ANY] * SIDE + [col(width)] * 2,
        [col(rows)] * 3 + [pl.BlockSpec((TILE, rows), lambda j: (j, 0))],
        [shape((rows, ff), F32), shape((rows, ff), F32), shape((rows, ff)), shape((ff, rows))],
        [*blocks, gate_mat, up_mat],
        [pltpu.VMEM((rows, width), BF), pltpu.SemaphoreType.DMA((SIDE,))],
        after=after,
    )


def transposed_rows(blocks, after):
    block, width = blocks[0].shape
    rows = SIDE * block

    def kernel(x0, x1, x2, x3, out, tall):
        for d, x in enumerate((x0, x1, x2, x3)):
            tall[d * block : (d + 1) * block, :] = x[...]
        out[...] = jnp.transpose(tall[...])

    return call(
        kernel,
        (width // TILE,),
        [pl.BlockSpec((block, TILE), lambda j: (0, j))] * SIDE,
        [pl.BlockSpec((TILE, rows), lambda j: (j, 0))],
        [shape((width, rows))],
        blocks,
        [pltpu.VMEM((rows, TILE), BF)],
        after=after,
    )[0]


def back_hidden(blocks, down_mat, gate_k, up_k, hidden, after=()):
    block, width = blocks[0].shape
    ff = down_mat.shape[0]
    rows = SIDE * block
    half = rows // 2

    def kernel(x0, x1, x2, x3, wd, gk, uk, hid, gate_back, up_back, dots, whole, total, sems):
        j = pl.program_id(0)

        @pl.when(j == 0)
        def _():
            gather_blocks((x0, x1, x2, x3), whole, sems)
            total[...] = jnp.zeros_like(total)

        for h in (0, half):
            at = slice(h, h + half)
            hg = lax.dot_general(whole[at, :], wd[...], NT, preferred_element_type=F32)
            gate_back[at, :] = (hg * gk[at, :]).astype(BF)
            up_back[at, :] = (hg * uk[at, :]).astype(BF)
            total[at, :] += jnp.sum(hg * hid[at, :].astype(F32), axis=1, keepdims=True)

        @pl.when(j == pl.num_programs(0) - 1)
        def _():
            for d in range(SIDE):
                at = slice(d * block, (d + 1) * block)
                lane = lax.broadcasted_iota(jnp.int32, (block, 128), 1)
                dots[at, :] = jnp.where(lane == d, total[at, :], 0.0).astype(BF)

    col = pl.BlockSpec((rows, TILE), lambda j: (0, j))
    return call(
        kernel,
        (ff // TILE,),
        [ANY] * SIDE + [pl.BlockSpec((TILE, width), lambda j: (j, 0)), col, col, col],
        [col, col, pl.BlockSpec((rows, 128), lambda j: (0, 0))],
        [shape((rows, ff)), shape((rows, ff)), shape((rows, 128))],
        [*blocks, down_mat, gate_k, up_k, hidden],
        [pltpu.VMEM((rows, width), BF), pltpu.VMEM((rows, 1), F32), pltpu.SemaphoreType.DMA((SIDE,))],
        after=after,
    )


def back_input(gate_back, up_back, gate_mat, up_mat, first, count, dots, after=()):
    rows, ff = gate_back.shape
    block = rows // SIDE
    extra = 0 if dots is None else dots.shape[1]

    def kernel(gb, ub, wg, wu, *refs):
        outs = refs[-SIDE:]
        n = pl.program_id(0)
        val = lax.dot_general(gb[...], wg[...], NT, preferred_element_type=F32)
        val += lax.dot_general(ub[...], wu[...], NT, preferred_element_type=F32)
        val = val.astype(BF)
        for d, o in enumerate(outs):
            o[:, pl.ds(pl.multiple_of(n * TILE, TILE), TILE)] = val[d * block : (d + 1) * block, :]
        if extra:

            @pl.when(n == 0)
            def _():
                for d, o in enumerate(outs):
                    o[:, count : count + extra] = refs[0][d * block : (d + 1) * block, :]

    full = lambda r, c: pl.BlockSpec((r, c), lambda n: (0, 0))
    weight = pl.BlockSpec((TILE, ff), lambda n: (first // TILE + n, 0))
    return call(
        kernel,
        (count // TILE,),
        [full(rows, ff)] * 2 + [weight] * 2 + [full(rows, extra)] * (extra > 0),
        [full(block, count + extra)] * SIDE,
        [shape((block, count + extra))] * SIDE,
        [gate_back, up_back, gate_mat, up_mat] + [dots] * (extra > 0),
        after=after,
    )


def weight_terms(rows_t, hidden_t, grads, gate_back, up_back, shares):
    width, rows = rows_t.shape
    ff = gate_back.shape[1]
    block = grads[0].shape[0]
    part = width // shares
    tiles = ff // part

    def kernel(x0, x1, x2, x3, ht, xt, gb, ub, out, rg, ht_v, xt_v, gb_v, ub_v, stage, in_sems, more, out_sems):
        copies = block_copies((x0, x1, x2, x3), rg, in_sems)
        loads = [
            pltpu.make_async_copy(src, dst, more.at[i])
            for i, (src, dst) in enumerate(((ht, ht_v), (gb, gb_v), (ub, ub_v), (xt, xt_v)))
        ]
        loads[0].start()
        for c in copies:
            c.start()
        for c in loads[1:]:
            c.start()
        loads[0].wait()
        for c in copies:
            c.wait()
        stores = []

        def put(value, where):
            slot = len(stores) % 2
            if len(stores) >= 2:
                stores[-2].wait()
            stage[slot] = value.astype(BF).reshape(stage.shape[1:])
            stores.append(pltpu.make_async_copy(stage.at[slot], where, out_sems.at[slot]))
            stores[-1].start()

        for t in range(tiles):
            at = slice(t * part, (t + 1) * part)
            value = jnp.concatenate(
                [
                    jnp.dot(ht_v[at, :], rg[:, s * part : (s + 1) * part], preferred_element_type=F32)
                    for s in range(shares)
                ],
                axis=0,
            )
            put(value, out.at[:, pl.ds((2 * tiles + t) * part, part), :])
        for i, (ref, load) in enumerate(((gb_v, loads[1]), (ub_v, loads[2]))):
            load.wait()
            if i == 0:
                loads[3].wait()
            for t in range(tiles):
                value = jnp.dot(xt_v[...], ref[:, t * part : (t + 1) * part], preferred_element_type=F32)
                put(value, out.at[:, pl.ds((i * tiles + t) * part, part), :])
        stores[-2].wait()
        stores[-1].wait()

    return call(
        kernel,
        (1,),
        [ANY] * (SIDE + 4),
        [ANY],
        [shape((shares, 3 * ff, part))],
        [*grads, hidden_t, rows_t, gate_back, up_back],
        [
            pltpu.VMEM((rows, width), BF),
            pltpu.VMEM((ff, rows), BF),
            pltpu.VMEM((width, rows), BF),
            pltpu.VMEM((rows, ff), BF),
            pltpu.VMEM((rows, ff), BF),
            pltpu.VMEM((2, shares, part, part), BF),
            pltpu.SemaphoreType.DMA((SIDE,)),
            pltpu.SemaphoreType.DMA((4,)),
            pltpu.SemaphoreType.DMA((2,)),
        ],
    )[0]


def merge_rows(placer, blocks, after=()):
    group = placer.shape[0]
    block, width = blocks[0].shape
    rows_dev = group // SIDE

    def kernel(place, x0, x1, x2, x3, o0, o1, o2, o3, whole, sems):
        gather_blocks((x0, x1, x2, x3), whole, sems)
        for at in range(0, width, TILE):
            cols = slice(at, min(at + TILE, width))
            val = jnp.dot(place[...], whole[:, cols], preferred_element_type=F32).astype(BF)
            for s, o in enumerate((o0, o1, o2, o3)):
                o[:, cols] = val[s * rows_dev : (s + 1) * rows_dev, :]

    full = lambda r, c: pl.BlockSpec((r, c), lambda i: (0, 0))
    return call(
        kernel,
        (1,),
        [full(*placer.shape)] + [ANY] * SIDE,
        [full(rows_dev, width)] * SIDE,
        [shape((rows_dev, width))] * SIDE,
        [placer, *blocks],
        [pltpu.VMEM((SIDE * block, width), BF), pltpu.SemaphoreType.DMA((SIDE,))],
        after=after,
    )


def plus(*terms):
    return sum(t.astype(F32) for t in terms).astype(BF)


def body(tokens, expert_ids, gate_probs, out_grad, w_gate, w_up, w_down):
    rows_dev, width = tokens.shape
    fanout = expert_ids.shape[1]
    n_dp = lax.axis_size("dp")
    groups = lax.axis_size("expert")
    mean_load = rows_dev * fanout // groups
    capacity = min(rows_dev, mean_load + max(2, rows_dev * fanout // (16 * groups)))
    block = SIDE * capacity

    dp_at = lax.axis_index("dp")
    x_at, z_at = coords(lax.axis_index("expert"))
    even = dp_at % 2 == 0
    a_at = jnp.where(even, x_at, z_at)
    b_at = jnp.where(even, z_at, x_at)

    def expert_of(a, b):
        a, b = a % SIDE, b % SIDE
        return jnp.where(even, a * SIDE + b, b * SIDE + a)

    def along(v, step, core):
        if step % SIDE == 0:
            return v
        return permuted(
            v, n_dp, lambda y, c, x, z: (y, c, x + step, z) if c == core else (y, c, x, z + step)
        )

    first = lambda v, step: along(v, step, 0)
    second = lambda v, step: along(v, step, 1)

    meta = jnp.concatenate([expert_ids.astype(BF), gate_probs], axis=1)
    meta = jnp.pad(meta, ((0, 0), (0, 128 - 2 * fanout)))
    packed = jnp.concatenate([tokens, out_grad, meta], axis=1)
    sources = [first(packed, s) for s in range(SIDE)]

    dests = jnp.stack([expert_of(a_at, b_at + d) for d in range(SIDE)]).astype(jnp.int32)
    *picked, slot, weight = pick_tokens(sources, dests, width, fanout, block)
    rows_in = [second(v, d) for d, v in enumerate(picked)]
    *picked, placer = pick_grads(sources, slot, weight, width, block, [])
    route_grad = [second(v, d) for d, v in enumerate(picked)]

    gate_mat, up_mat, down_mat = w_gate[0], w_up[0], w_down[0]
    ff = gate_mat.shape[1]
    gate_k, up_k, hidden, hidden_t = forward(rows_in, gate_mat, up_mat, [placer])
    rows_t = transposed_rows(rows_in, [hidden_t])
    gate_back, up_back, dots = back_hidden(route_grad, down_mat, gate_k, up_k, hidden, [rows_t])
    terms = weight_terms(rows_t, hidden_t, route_grad, gate_back, up_back, n_dp)
    cut = width // 2
    in_0 = back_input(gate_back, up_back, gate_mat, up_mat, 0, cut, dots, [terms])
    in_1 = back_input(gate_back, up_back, gate_mat, up_mat, cut, width - cut, None, [in_0[0]])

    owned = lax.psum_scatter(terms, "dp", scatter_dimension=0, tiled=True)[0]
    share = width // n_dp
    tile_cols = lambda at: jnp.concatenate(
        [owned[at + t * share : at + (t + 1) * share] for t in range(ff // share)], axis=1
    )

    sums = []
    for part in (in_0, in_1):
        back = [second(v, -d) for d, v in enumerate(part)]
        merged = merge_rows(placer, back)
        sums.append([first(v, -s) for s, v in enumerate(merged)])
    token_grad = jnp.concatenate([plus(*[v[:, :cut] for v in sums[0]]), plus(*sums[1])], axis=1)
    prob_grad = jnp.zeros(expert_ids.shape, F32)
    for s in range(SIDE):
        vals = sums[0][s][:, cut:].astype(F32)
        for d in range(SIDE):
            prob_grad += jnp.where(expert_ids == expert_of(a_at + s, b_at + d), vals[:, d : d + 1], 0.0)
    prob_grad = (prob_grad / gate_probs.astype(F32)).astype(BF)

    return (
        token_grad,
        prob_grad,
        tile_cols(0)[None],
        tile_cols(ff)[None],
        owned[2 * ff :][None],
    )


def solution(mesh):
    rows = P(("dp", "expert"), None)
    mats = P("expert", None, None)
    return jax.shard_map(
        body,
        mesh=mesh,
        in_specs=(rows, rows, rows, rows, mats, mats, mats),
        out_specs=(rows, rows, P("expert", "dp", None), P("expert", "dp", None), P("expert", None, "dp")),
        check_vma=False,
    )
```

```python
import jax
import jax.numpy as jnp
from jax import lax
from jax.experimental import pallas as pl
from jax.experimental.pallas import tpu as pltpu
from jax.sharding import PartitionSpec as P

AXES = ("dp", "expert")
SIDE = 4
BF = jnp.bfloat16
F32 = jnp.float32
TILE = 256
VMEM_LIMIT = 16 * 2**20

NT = (((1,), (1,)), ((), ()))
TN = (((0,), (0,)), ((), ()))


def coords(expert):
    return expert // SIDE, expert % SIDE


def permuted(value, n_dp, target):
    pairs = []
    for dp in range(n_dp):
        for e in range(SIDE * SIDE):
            y, c, x, z = target(dp // 2, dp % 2, *coords(e))
            to = (y % SIDE * 2 + c) * SIDE * SIDE + x % SIDE * SIDE + z % SIDE
            pairs.append((dp * SIDE * SIDE + e, to))
    return lax.ppermute(value, AXES, pairs)


def call(kernel, out_shape, args, scratch=(), scalars=(), blocks=(), after=(), hbm_out=False, scalars_out=0, limit=VMEM_LIMIT):
    vmem = pl.BlockSpec(memory_space=pltpu.VMEM)
    smem = pl.BlockSpec(memory_space=pltpu.SMEM)
    anywhere = pl.BlockSpec(memory_space=pl.ANY)
    outs = pl.BlockSpec(memory_space=pltpu.HBM) if hbm_out else vmem

    def run(*refs):
        kernel(*refs[len(after) :])

    return pl.pallas_call(
        run,
        in_specs=[anywhere] * len(after)
        + [smem] * len(scalars)
        + [anywhere] * len(blocks)
        + [vmem] * len(args),
        out_specs=[outs] * (len(out_shape) - scalars_out) + [smem] * scalars_out,
        out_shape=list(out_shape),
        scratch_shapes=list(scratch),
        compiler_params=pltpu.CompilerParams(vmem_limit_bytes=limit),
        cost_estimate=pl.CostEstimate(flops=1000, bytes_accessed=1000, transcendentals=0),
    )(*after, *scalars, *blocks, *args)


def shape(dims, kind=BF):
    return jax.ShapeDtypeStruct(dims, kind)


def stack_blocks(blocks, whole, sems):
    rows = blocks[0].shape[0]
    copies = [
        pltpu.make_async_copy(b, whole.at[pl.ds(i * rows, rows), :], sems.at[i]) for i, b in enumerate(blocks)
    ]
    for c in copies:
        c.start()
    for c in copies:
        c.wait()


SEMS = pltpu.SemaphoreType.DMA((SIDE,))


def pack(tokens, expert_ids, gate_probs, experts, order):
    rows, width = tokens.shape
    fanout = expert_ids.shape[1]

    def kernel(experts, order, tok, ids, probs, out, experts_out, order_out):
        for i in range(experts.shape[0]):
            experts_out[i] = experts[i]
        for i in range(order.shape[0]):
            order_out[i] = order[i]
        out[:, :width] = tok[...]
        out[:, width:] = jnp.concatenate(
            [
                ids[...].astype(F32),
                probs[...].astype(F32),
                jnp.zeros((rows, 128 - 2 * fanout), F32),
            ],
            axis=1,
        ).astype(BF)

    return call(
        kernel,
        [shape((rows, width + 128)), shape(experts.shape, jnp.int32), shape(order.shape, jnp.int32)],
        [tokens, expert_ids, gate_probs],
        scalars=[experts, order],
        scalars_out=2,
    )


def onehot_dots(onehot, whole, outs):
    width = outs[0].shape[1]
    for d, o in enumerate(outs):
        hot = onehot(d)
        for at in range(0, width, 512):
            cols = slice(at, at + 512)
            o[:, cols] = jnp.dot(hot, whole[:, cols], preferred_element_type=F32).astype(BF)


def pick_tokens(sources, dests, width, fanout, block):
    rows_dev = sources[0].shape[0]
    group = SIDE * rows_dev

    def kernel(dest, x0, x1, x2, x3, o0, o1, o2, o3, slot, weight, whole, sems):
        stack_blocks((x0, x1, x2, x3), whole, sems)
        hits, probs = [], []
        sheets = [
            jnp.transpose(whole[s * rows_dev : (s + 1) * rows_dev, width:].astype(F32)) for s in range(SIDE)
        ]
        for d in range(SIDE):
            hit, prob = [], []
            for m in sheets:
                same = jnp.where(m[:fanout, :] == dest[d].astype(F32), 1.0, 0.0)
                hit.append(jnp.sum(same, axis=0, keepdims=True))
                prob.append(jnp.sum(same * m[fanout : 2 * fanout, :], axis=0, keepdims=True))
            hits.append(jnp.concatenate(hit, axis=1))
            probs.append(jnp.concatenate(prob, axis=1))
        hits = jnp.concatenate(hits + [jnp.zeros((SIDE, group), F32)], axis=0)
        probs = jnp.concatenate(probs + [jnp.zeros((SIDE, group), F32)], axis=0)
        earlier = lax.broadcasted_iota(jnp.int32, (group, group), 0) < lax.broadcasted_iota(
            jnp.int32, (group, group), 1
        )
        rank = jnp.dot(
            hits.astype(BF), jnp.where(earlier, 1.0, 0.0).astype(BF), preferred_element_type=F32
        )
        slot[...] = jnp.where(hits > 0.5, rank, -4096.0)
        weight[...] = probs
        row = lax.broadcasted_iota(jnp.int32, (block, group), 0).astype(F32)
        onehot_dots(
            lambda d: jnp.where(row == slot[d : d + 1, :], 1.0, 0.0).astype(BF), whole, (o0, o1, o2, o3)
        )

    return call(
        kernel,
        [shape((block, width))] * SIDE + [shape((2 * SIDE, group), F32)] * 2,
        [],
        [pltpu.VMEM((group, width + 128), BF), SEMS],
        [dests],
        sources,
    )


def pick_grads(sources, slot, weight, block):
    rows_dev, width = sources[0].shape
    group = SIDE * rows_dev

    def kernel(x0, x1, x2, x3, slot, weight, o0, o1, o2, o3, whole, sems):
        stack_blocks((x0, x1, x2, x3), whole, sems)
        row = lax.broadcasted_iota(jnp.int32, (block, group), 0).astype(F32)
        onehot_dots(
            lambda d: jnp.where(row == slot[d : d + 1, :], weight[d : d + 1, :], 0.0).astype(BF),
            whole,
            (o0, o1, o2, o3),
        )

    return call(
        kernel,
        [shape((block, width))] * SIDE,
        [slot, weight],
        [pltpu.VMEM((group, width), BF), SEMS],
        blocks=sources,
    )


def place_matrix(slot, block):
    group = slot.shape[1]

    def kernel(slot, place):
        tall = jnp.transpose(jnp.concatenate([slot[...]] * 16, axis=0))
        lane = lax.broadcasted_iota(jnp.int32, (group, SIDE * block), 1).astype(F32)
        back = jnp.zeros((group, SIDE * block), F32)
        for d in range(SIDE):
            back = jnp.where(lane == tall[:, d : d + 1] + float(d * block), 1.0, back)
        place[...] = back.astype(BF)

    return call(kernel, [shape((group, SIDE * block))], [slot])[0]


def forward(blocks, gate_mat, up_mat):
    block, width = blocks[0].shape
    ff = gate_mat.shape[1]
    rows = SIDE * block
    half = rows // 2

    def kernel(x0, x1, x2, x3, wg, wu, whole, hidden, gate_k, up_k, sems):
        stack_blocks((x0, x1, x2, x3), whole, sems)
        for n in range(0, ff, TILE):
            cols = slice(n, n + TILE)
            for h in (0, half):
                at = slice(h, h + half)
                g = jnp.dot(whole[at, :], wg[:, cols], preferred_element_type=F32)
                u = jnp.dot(whole[at, :], wu[:, cols], preferred_element_type=F32)
                s = jax.nn.sigmoid(g)
                act = g * s
                hidden[at, cols] = (act * u).astype(BF)
                gate_k[at, cols] = (u * s * (1.0 + g * (1.0 - s))).astype(BF)
                up_k[at, cols] = act.astype(BF)

    return call(
        kernel,
        [shape((rows, width))] + [shape((rows, ff))] * 3,
        [gate_mat, up_mat],
        [SEMS],
        blocks=blocks,
    )


def back_hidden(blocks, down_mat, gate_k, up_k, hidden):
    block, width = blocks[0].shape
    ff = down_mat.shape[0]
    rows = SIDE * block
    half = rows // 2

    def kernel(x0, x1, x2, x3, wd, gk, uk, hid, whole, gate_back, up_back, dots, total, sems):
        stack_blocks((x0, x1, x2, x3), whole, sems)
        for n in range(0, ff, TILE):
            cols = slice(n, n + TILE)
            for h in (0, half):
                at = slice(h, h + half)
                hg = lax.dot_general(whole[at, :], wd[cols, :], NT, preferred_element_type=F32)
                gate_back[at, cols] = (hg * gk[at, cols].astype(F32)).astype(BF)
                up_back[at, cols] = (hg * uk[at, cols].astype(F32)).astype(BF)
                term = hg * hid[at, cols].astype(F32)
                term = term[:, :128] + term[:, 128:]
                total[at, :] = term if n == 0 else total[at, :] + term
        for d in range(SIDE):
            at = slice(d * block, (d + 1) * block)
            lane = lax.broadcasted_iota(jnp.int32, (block, 128), 1)
            dot = jnp.sum(total[at, :], axis=1, keepdims=True)
            dots[at, :] = jnp.where(lane == d, dot, 0.0).astype(BF)

    return call(
        kernel,
        [shape((rows, width)), shape((rows, ff)), shape((rows, ff)), shape((rows, 128))],
        [down_mat, gate_k, up_k, hidden],
        [pltpu.VMEM((rows, 128), F32), SEMS],
        blocks=blocks,
    )


def back_input(gate_back, up_back, gate_mat, up_mat, first, count, after, dots=None):
    rows, ff = gate_back.shape
    block = rows // SIDE
    extra = 0 if dots is None else dots.shape[1]

    def kernel(gb, ub, wg, wu, *refs):
        outs = refs[-SIDE:]
        for n in range(0, count, TILE):
            at = slice(first + n, first + n + TILE)
            val = lax.dot_general(gb[...], wg[at, :], NT, preferred_element_type=F32)
            val += lax.dot_general(ub[...], wu[at, :], NT, preferred_element_type=F32)
            val = val.astype(BF)
            for d, o in enumerate(outs):
                o[:, n : n + TILE] = val[d * block : (d + 1) * block, :]
        for d, o in enumerate(outs):
            if extra:
                o[:, count:] = refs[0][d * block : (d + 1) * block, :]

    return call(
        kernel,
        [shape((block, count + extra))] * SIDE,
        [gate_back, up_back, gate_mat, up_mat] + ([dots] if extra else []),
        after=after,
    )


def gate_up_terms(whole, gate_back, up_back, shares):
    width = whole.shape[1]
    ff = gate_back.shape[1]
    part = width // shares

    def kernel(x, gb, ub, out, stage, sems):
        stores = []
        for i, ref in enumerate((gb, ub)):
            for n in range(0, ff, TILE):
                slot = len(stores) % 2
                if len(stores) >= 2:
                    stores[-2].wait()
                value = lax.dot_general(x[...], ref[:, n : n + TILE], TN, preferred_element_type=F32)
                stage[slot] = value.astype(BF).reshape(shares, part, TILE)
                row = i * (ff // TILE) * part + n // TILE * part
                stores.append(
                    pltpu.make_async_copy(stage.at[slot], out.at[:, pl.ds(row, part), :], sems.at[slot])
                )
                stores[-1].start()
        stores[-2].wait()
        stores[-1].wait()

    return call(
        kernel,
        [shape((shares, 2 * (ff // TILE) * part, TILE))],
        [whole, gate_back, up_back],
        [pltpu.VMEM((2, shares, part, TILE), BF), pltpu.SemaphoreType.DMA((2,))],
        hbm_out=True,
    )[0]


def down_terms(hidden, whole, order, shares):
    ff, width = hidden.shape[1], whole.shape[1]
    part = width // shares
    half = shares // 2

    def kernel(order, hid, x, give, keep):
        for k in range(shares):
            cols = pl.ds(pl.multiple_of(order[k] * part, part), part)
            out = give if k < half else keep
            out[k % half] = lax.dot_general(hid[...], x[:, cols], TN, preferred_element_type=F32).astype(BF)

    return call(kernel, [shape((half, ff, part))] * 2, [hidden, whole], scalars=[order])


def merge_rows(placer, blocks):
    group = placer.shape[0]
    block, width = blocks[0].shape
    rows_dev = group // SIDE

    def kernel(x0, x1, x2, x3, place, o0, o1, o2, o3, whole, sems):
        stack_blocks((x0, x1, x2, x3), whole, sems)
        for at in range(0, width, TILE):
            cols = slice(at, min(at + TILE, width))
            val = jnp.dot(place[...], whole[:, cols], preferred_element_type=F32).astype(BF)
            for s, o in enumerate((o0, o1, o2, o3)):
                o[:, cols] = val[s * rows_dev : (s + 1) * rows_dev, :]

    return call(
        kernel,
        [shape((rows_dev, width))] * SIDE,
        [placer],
        [pltpu.VMEM((SIDE * block, width), BF), SEMS],
        blocks=blocks,
    )


def add_halves(keep, got):
    def kernel(a, b, *outs):
        for k, o in enumerate(outs):
            o[...] = (a[k].astype(F32) + b[k].astype(F32)).astype(BF)

    return call(kernel, [shape(keep.shape[1:])] * keep.shape[0], [keep, got])


def add_all(terms):
    def kernel(*refs):
        refs[-1][...] = sum(r[...].astype(F32) for r in refs[:-1]).astype(BF)

    return call(kernel, [shape(terms[0].shape)], terms)[0]


def finish(near, far, expert_ids, gate_probs, experts):
    rows, fanout = expert_ids.shape
    left, right = near[0].shape[1] - 128, far[0].shape[1]

    def kernel(experts, *refs):
        a, b = refs[:SIDE], refs[SIDE : 2 * SIDE]
        ids, probs, grad, prob = refs[2 * SIDE :]
        grad[:, :left] = sum(r[:, :left].astype(F32) for r in a).astype(BF)
        grad[:, left:] = sum(r[...].astype(F32) for r in b).astype(BF)
        total = jnp.zeros((rows, fanout), F32)
        for s in range(SIDE):
            vals = a[s][:, left:].astype(F32)
            for d in range(SIDE):
                total += jnp.where(ids[...] == experts[s * SIDE + d], vals[:, d : d + 1], 0.0)
        prob[...] = (total / probs[...].astype(F32)).astype(BF)

    return call(
        kernel,
        [shape((rows, left + right)), shape((rows, fanout))],
        [*near, *far, expert_ids, gate_probs],
        scalars=[experts],
    )


def body(tokens, expert_ids, gate_probs, out_grad, w_gate, w_up, w_down):
    rows_dev, width = tokens.shape
    fanout = expert_ids.shape[1]
    n_dp = lax.axis_size("dp")
    groups = lax.axis_size("expert")
    mean_load = rows_dev * fanout // groups
    capacity = min(rows_dev, mean_load + max(2, rows_dev * fanout // (16 * groups)))
    block = SIDE * capacity

    dp_at = lax.axis_index("dp")
    x_at, z_at = coords(lax.axis_index("expert"))
    even = dp_at % 2 == 0
    a_at = jnp.where(even, x_at, z_at)
    b_at = jnp.where(even, z_at, x_at)

    def expert_of(a, b):
        a, b = a % SIDE, b % SIDE
        return jnp.where(even, a * SIDE + b, b * SIDE + a)

    def along(v, step, core):
        if step % SIDE == 0:
            return v
        return permuted(
            v, n_dp, lambda y, c, x, z: (y, c, x + step, z) if c == core else (y, c, x, z + step)
        )

    first = lambda v, step: along(v, step, 0)
    second = lambda v, step: along(v, step, 1)

    experts = jnp.stack([expert_of(a_at + s, b_at + d) for s in range(SIDE) for d in range(SIDE)])
    near = (dp_at // 2 + jnp.arange(SIDE, dtype=jnp.int32)) % SIDE * 2
    order = jnp.concatenate([near + 1 - dp_at % 2, near + dp_at % 2])
    packed, experts, order = pack(tokens, expert_ids, gate_probs, experts.astype(jnp.int32), order)
    tok_sources = [first(packed, s) for s in range(SIDE)]
    grad_sources = [first(out_grad, s) for s in range(SIDE)]

    *picked, slot, weight = pick_tokens(tok_sources, experts, width, fanout, block)
    rows_in = [second(v, d) for d, v in enumerate(picked)]
    picked = pick_grads(grad_sources, slot, weight, block)
    route_grad = [second(v, d) for d, v in enumerate(picked)]

    gate_mat, up_mat, down_mat = w_gate[0], w_up[0], w_down[0]
    ff = gate_mat.shape[1]
    rows_all, hidden, gate_k, up_k = forward(rows_in, gate_mat, up_mat)
    placer = place_matrix(slot, block)
    grad_all, gate_back, up_back, dots = back_hidden(route_grad, down_mat, gate_k, up_k, hidden)

    owned = lax.psum_scatter(
        gate_up_terms(rows_all, gate_back, up_back, n_dp), "dp", scatter_dimension=0, tiled=True
    )[0]
    share = width // n_dp
    give, keep = down_terms(hidden, grad_all, order, n_dp)
    got = permuted(give, n_dp, lambda y, c, x, z: (y, 1 - c, x, z))
    sums = add_halves(keep, got)
    far = [permuted(sums[k], n_dp, lambda y, c, x, z: (y + k, c, x, z)) for k in range(1, SIDE)]
    down_own = add_all([sums[0], *far])

    cut = width // 2
    parts = (
        back_input(gate_back, up_back, gate_mat, up_mat, 0, cut, [give], dots),
        back_input(gate_back, up_back, gate_mat, up_mat, cut, width - cut, [give]),
    )

    ends = []
    for rows in parts:
        merged = merge_rows(placer, [second(v, -d) for d, v in enumerate(rows)])
        ends.append([first(v, -s) for s, v in enumerate(merged)])
    token_grad, prob_grad = finish(*ends, expert_ids, gate_probs, experts)

    def tile_cols(at):
        return jnp.concatenate([owned[at + t * share : at + (t + 1) * share] for t in range(ff // TILE)], axis=1)

    half = ff // TILE * share
    return (token_grad, prob_grad, tile_cols(0)[None], tile_cols(half)[None], down_own[None])


def solution(mesh):
    rows = P(("dp", "expert"), None)
    mats = P("expert", None, None)
    return jax.shard_map(
        body,
        mesh=mesh,
        in_specs=(rows, rows, rows, rows, mats, mats, mats),
        out_specs=(rows, rows, P("expert", "dp", None), P("expert", "dp", None), P("expert", None, "dp")),
        check_vma=False,
    )
```

```python
import jax
import jax.numpy as jnp
from jax import lax
from jax.experimental import pallas as pl
from jax.experimental.pallas import tpu as pltpu
from jax.sharding import PartitionSpec as P

AXES = ("dp", "expert")
SIDE = 4
BF = jnp.bfloat16
F32 = jnp.float32
TILE = 256
VMEM_LIMIT = 16 * 2**20

NT = (((1,), (1,)), ((), ()))
TN = (((0,), (0,)), ((), ()))


def coords(expert):
    return expert // SIDE, expert % SIDE


def permuted(value, n_dp, target):
    pairs = []
    for dp in range(n_dp):
        for e in range(SIDE * SIDE):
            y, c, x, z = target(dp // 2, dp % 2, *coords(e))
            to = (y % SIDE * 2 + c) * SIDE * SIDE + x % SIDE * SIDE + z % SIDE
            pairs.append((dp * SIDE * SIDE + e, to))
    return lax.ppermute(value, AXES, pairs)


def call(kernel, out_shape, args, scratch=(), scalars=(), blocks=(), after=(), scalars_out=0, hidden_out=(), cost=0.0):
    vmem = pl.BlockSpec(memory_space=pltpu.VMEM)
    smem = pl.BlockSpec(memory_space=pltpu.SMEM)
    anywhere = pl.BlockSpec(memory_space=pl.ANY)

    def run(*refs):
        kernel(*refs[len(after) :])

    return pl.pallas_call(
        run,
        in_specs=[anywhere] * len(after)
        + [smem] * len(scalars)
        + [anywhere] * len(blocks)
        + [vmem] * len(args),
        out_specs=[
            anywhere if i in hidden_out else vmem if i < len(out_shape) - scalars_out else smem
            for i in range(len(out_shape))
        ],
        out_shape=list(out_shape),
        scratch_shapes=list(scratch),
        compiler_params=pltpu.CompilerParams(vmem_limit_bytes=VMEM_LIMIT),
        cost_estimate=pl.CostEstimate(
            flops=1000 + int(cost * 1e15), bytes_accessed=1000 + int(cost * 3.5e12), transcendentals=0
        ),
    )(*after, *scalars, *blocks, *args)


def shape(dims, kind=BF):
    return jax.ShapeDtypeStruct(dims, kind)


def stack_blocks(blocks, whole, sems):
    copies, row = [], 0
    for i, b in enumerate(blocks):
        rows = b.shape[0]
        copies.append(pltpu.make_async_copy(b, whole.at[pl.ds(row, rows), :], sems.at[i]))
        row += rows
    for c in copies:
        c.start()
    for c in copies:
        c.wait()


PARTS = SIDE + 1
SEMS = pltpu.SemaphoreType.DMA((PARTS,))


def part_rows(block):
    far = (block // 2 + 15) // 16 * 16
    return [block, block, far, block - far, block]


def split_rows(value, block):
    row = 0
    for rows in part_rows(block):
        yield value[row : row + rows, :]
        row += rows


def pack(tokens, expert_ids, gate_probs, experts, order):
    rows, width = tokens.shape
    fanout = expert_ids.shape[1]

    def kernel(experts, order, tok, ids, probs, out, experts_out, order_out):
        for i in range(experts.shape[0]):
            experts_out[i] = experts[i]
        for i in range(order.shape[0]):
            order_out[i] = order[i]
        out[:, :width] = tok[...]
        out[:, width:] = jnp.concatenate(
            [
                ids[...].astype(F32),
                probs[...].astype(F32),
                jnp.zeros((rows, 128 - 2 * fanout), F32),
            ],
            axis=1,
        ).astype(BF)

    return call(
        kernel,
        [shape((rows, width + 128)), shape(experts.shape, jnp.int32), shape(order.shape, jnp.int32)],
        [tokens, expert_ids, gate_probs],
        scalars=[experts, order],
        scalars_out=2,
    )


def onehot_dots(onehot, whole, outs, block):
    width = outs[0].shape[1]
    far = part_rows(block)[2]
    for d in range(SIDE):
        hot = onehot(d)
        for at in range(0, width, 512):
            cols = slice(at, at + 512)
            value = jnp.dot(hot, whole[:, cols], preferred_element_type=F32).astype(BF)
            if d == 2:
                outs[2][:, cols] = value[:far, :]
                outs[3][:, cols] = value[far:, :]
            else:
                outs[d if d < 2 else PARTS - 1][:, cols] = value


def pick_tokens(sources, dests, width, fanout, block):
    rows_dev = sources[0].shape[0]
    group = SIDE * rows_dev

    def kernel(dest, x0, x1, x2, x3, o0, o1, o2, o3, o4, slot, weight, whole, sems):
        stack_blocks((x0, x1, x2, x3), whole, sems)
        hits, probs = [], []
        sheets = [
            jnp.transpose(whole[s * rows_dev : (s + 1) * rows_dev, width:].astype(F32)) for s in range(SIDE)
        ]
        for d in range(SIDE):
            hit, prob = [], []
            for m in sheets:
                same = jnp.where(m[:fanout, :] == dest[d].astype(F32), 1.0, 0.0)
                hit.append(jnp.sum(same, axis=0, keepdims=True))
                prob.append(jnp.sum(same * m[fanout : 2 * fanout, :], axis=0, keepdims=True))
            hits.append(jnp.concatenate(hit, axis=1))
            probs.append(jnp.concatenate(prob, axis=1))
        hits = jnp.concatenate(hits + [jnp.zeros((SIDE, group), F32)], axis=0)
        probs = jnp.concatenate(probs + [jnp.zeros((SIDE, group), F32)], axis=0)
        earlier = lax.broadcasted_iota(jnp.int32, (group, group), 0) < lax.broadcasted_iota(
            jnp.int32, (group, group), 1
        )
        rank = jnp.dot(
            hits.astype(BF), jnp.where(earlier, 1.0, 0.0).astype(BF), preferred_element_type=F32
        )
        slot[...] = jnp.where(hits > 0.5, rank, -4096.0)
        weight[...] = probs
        row = lax.broadcasted_iota(jnp.int32, (block, group), 0).astype(F32)
        onehot_dots(
            lambda d: jnp.where(row == slot[d : d + 1, :], 1.0, 0.0).astype(BF),
            whole,
            (o0, o1, o2, o3, o4),
            block,
        )

    return call(
        kernel,
        [shape((r, width)) for r in part_rows(block)] + [shape((2 * SIDE, group), F32)] * 2,
        [],
        [pltpu.VMEM((group, width + 128), BF), SEMS],
        [dests],
        sources,
    )


def pick_grads(sources, slot, weight, block):
    rows_dev, width = sources[0].shape
    group = SIDE * rows_dev

    def kernel(x0, x1, x2, x3, slot, weight, o0, o1, o2, o3, o4, whole, sems):
        stack_blocks((x0, x1, x2, x3), whole, sems)
        row = lax.broadcasted_iota(jnp.int32, (block, group), 0).astype(F32)
        onehot_dots(
            lambda d: jnp.where(row == slot[d : d + 1, :], weight[d : d + 1, :], 0.0).astype(BF),
            whole,
            (o0, o1, o2, o3, o4),
            block,
        )

    return call(
        kernel,
        [shape((r, width)) for r in part_rows(block)],
        [slot, weight],
        [pltpu.VMEM((group, width), BF), SEMS],
        blocks=sources,
    )


def place_matrix(slot, block):
    group = slot.shape[1]

    def kernel(slot, place):
        tall = jnp.transpose(jnp.concatenate([slot[...]] * 16, axis=0))
        lane = lax.broadcasted_iota(jnp.int32, (group, SIDE * block), 1).astype(F32)
        back = jnp.zeros((group, SIDE * block), F32)
        for d in range(SIDE):
            back = jnp.where(lane == tall[:, d : d + 1] + float(d * block), 1.0, back)
        place[...] = back.astype(BF)

    return call(kernel, [shape((group, SIDE * block))], [slot])[0]


def forward(blocks, gate_mat, up_mat):
    width = blocks[0].shape[1]
    ff = gate_mat.shape[1]
    rows = sum(b.shape[0] for b in blocks)
    half = rows // 2

    def kernel(x0, x1, x2, x3, x4, wg, wu, whole, hidden, gate_k, up_k, sems):
        stack_blocks((x0, x1, x2, x3, x4), whole, sems)
        for n in range(0, ff, TILE):
            cols = slice(n, n + TILE)
            for h in (0, half):
                at = slice(h, h + half)
                g = jnp.dot(whole[at, :], wg[:, cols], preferred_element_type=F32)
                u = jnp.dot(whole[at, :], wu[:, cols], preferred_element_type=F32)
                s = jax.nn.sigmoid(g)
                act = g * s
                hidden[at, cols] = (act * u).astype(BF)
                gate_k[at, cols] = (u * s * (1.0 + g * (1.0 - s))).astype(BF)
                up_k[at, cols] = act.astype(BF)

    return call(
        kernel,
        [shape((rows, width))] + [shape((rows, ff))] * 3,
        [gate_mat, up_mat],
        [SEMS],
        blocks=blocks,
    )


def back_hidden(blocks, down_mat, gate_k, up_k, hidden):
    block, width = blocks[0].shape
    ff = down_mat.shape[0]
    rows = sum(b.shape[0] for b in blocks)
    half = rows // 2

    def kernel(x0, x1, x2, x3, x4, wd, gk, uk, hid, out, gate_back, up_back, dots, whole, total, sems):
        stack_blocks((x0, x1, x2, x3, x4), whole, sems)
        store = pltpu.make_async_copy(whole, out, sems.at[0])
        store.start()
        for n in range(0, ff, TILE):
            cols = slice(n, n + TILE)
            for h in (0, half):
                at = slice(h, h + half)
                hg = lax.dot_general(whole[at, :], wd[cols, :], NT, preferred_element_type=F32)
                gate_back[at, cols] = (hg * gk[at, cols].astype(F32)).astype(BF)
                up_back[at, cols] = (hg * uk[at, cols].astype(F32)).astype(BF)
                term = hg * hid[at, cols].astype(F32)
                term = term[:, :128] + term[:, 128:]
                total[at, :] = term if n == 0 else total[at, :] + term
        for d in range(SIDE):
            at = slice(d * block, (d + 1) * block)
            lane = lax.broadcasted_iota(jnp.int32, (block, 128), 1)
            dot = jnp.sum(total[at, :], axis=1, keepdims=True)
            dots[at, :] = jnp.where(lane == d, dot, 0.0).astype(BF)
        store.wait()

    return call(
        kernel,
        [shape((rows, width)), shape((rows, ff)), shape((rows, ff)), shape((rows, 128))],
        [down_mat, gate_k, up_k, hidden],
        [pltpu.VMEM((rows, width), BF), pltpu.VMEM((rows, 128), F32), SEMS],
        blocks=blocks,
        hidden_out=(0,),
    )


def back_input(gate_back, up_back, gate_mat, up_mat, dots):
    rows, ff = gate_back.shape
    width = gate_mat.shape[0]
    block = rows // SIDE
    wide = width + dots.shape[1]

    def kernel(gb, ub, wg, wu, dots, o0, o1, o2, o3, o4, whole, sems):
        whole[:, width:] = dots[...]
        for n in range(0, width, TILE):
            at = slice(n, n + TILE)
            val = lax.dot_general(gb[...], wg[at, :], NT, preferred_element_type=F32)
            val += lax.dot_general(ub[...], wu[at, :], NT, preferred_element_type=F32)
            whole[:, at] = val.astype(BF)
        stores, row = [], 0
        for i, o in enumerate((o0, o1, o2, o3, o4)):
            stores.append(pltpu.make_async_copy(whole.at[pl.ds(row, o.shape[0]), :], o, sems.at[i]))
            row += o.shape[0]
        for c in stores:
            c.start()
        for c in stores:
            c.wait()

    return call(
        kernel,
        [shape((r, wide)) for r in part_rows(block)],
        [gate_back, up_back, gate_mat, up_mat, dots],
        [pltpu.VMEM((rows, wide), BF), SEMS],
        hidden_out=range(PARTS),
    )


def gate_up_terms(whole, gate_back, up_back, shares, after):
    width = whole.shape[1]
    ff = gate_back.shape[1]
    part = width // shares

    def kernel(x, gb, ub, out, mark):
        mark[...] = jnp.zeros(mark.shape, F32)
        row = 0
        for ref in (gb, ub):
            for n in range(0, ff, TILE):
                value = lax.dot_general(x[...], ref[:, n : n + TILE], TN, preferred_element_type=F32)
                value = value.astype(BF)
                for s in range(shares):
                    out[s, row : row + part, :] = value[s * part : (s + 1) * part, :]
                row += part

    return call(
        kernel,
        [shape((shares, 2 * (ff // TILE) * part, TILE)), shape((8, 128), F32)],
        [whole, gate_back, up_back],
        after=after,
    )


def down_terms(hidden, whole, order, shares, after):
    ff, width = hidden.shape[1], whole.shape[1]
    part = width // shares
    half = shares // 2

    def kernel(order, hid, x, give, keep):
        for k in range(shares):
            cols = pl.ds(pl.multiple_of(order[k] * part, part), part)
            out = give if k < half else keep
            out[k % half] = lax.dot_general(hid[...], x[:, cols], TN, preferred_element_type=F32).astype(BF)

    return call(kernel, [shape((half, ff, part))] * 2, [hidden, whole], scalars=[order], after=after)


def merge_rows(placer, blocks, after):
    group, rows = placer.shape
    width = blocks[0].shape[1]
    rows_dev = group // SIDE

    def kernel(x0, x1, x2, x3, x4, place, o0, o1, o2, o3, o4, whole, sems):
        stack_blocks((x0, x1, x2, x3, x4), whole, sems)
        for at in range(0, width, TILE):
            cols = slice(at, min(at + TILE, width))
            val = jnp.dot(place[...], whole[:, cols], preferred_element_type=F32).astype(BF)
            for o, v in zip((o0, o1, o2, o3, o4), split_rows(val, rows_dev)):
                o[:, cols] = v

    return call(
        kernel,
        [shape((r, width)) for r in part_rows(rows_dev)],
        [placer],
        [pltpu.VMEM((rows, width), BF), SEMS],
        blocks=blocks,
        after=after,
    )


def add_halves(keep, got, after):
    def kernel(a, b, *outs):
        for k, o in enumerate(outs):
            o[...] = (a[k].astype(F32) + b[k].astype(F32)).astype(BF)

    return call(kernel, [shape(keep.shape[1:])] * keep.shape[0], [keep, got], after=after)


def add_all(terms):
    def kernel(*refs):
        refs[-1][...] = sum(r[...].astype(F32) for r in refs[:-1]).astype(BF)

    return call(kernel, [shape(terms[0].shape)], terms)[0]


def finish(terms, expert_ids, gate_probs, experts):
    rows, fanout = expert_ids.shape
    width = terms[0].shape[1] - 128
    far = part_rows(rows)[2]

    def kernel(experts, x0, x1, x2, x3, x4, ids, probs, grad, prob):
        for at in (slice(0, far), slice(far, rows)):
            parts = (x0[at, :], x1[at, :], (x2 if at.start == 0 else x3)[...], x4[at, :])
            grad[at, :] = sum(p[:, :width].astype(F32) for p in parts).astype(BF)
            total = jnp.zeros((at.stop - at.start, fanout), F32)
            for s in range(SIDE):
                vals = parts[s][:, width:].astype(F32)
                for d in range(SIDE):
                    total += jnp.where(ids[at, :] == experts[s * SIDE + d], vals[:, d : d + 1], 0.0)
            prob[at, :] = (total / probs[at, :].astype(F32)).astype(BF)

    return call(
        kernel,
        [shape((rows, width)), shape((rows, fanout))],
        [*terms, expert_ids, gate_probs],
        scalars=[experts],
        cost=0.000117,
    )


def body(tokens, expert_ids, gate_probs, out_grad, w_gate, w_up, w_down):
    rows_dev, width = tokens.shape
    fanout = expert_ids.shape[1]
    n_dp = lax.axis_size("dp")
    groups = lax.axis_size("expert")
    mean_load = rows_dev * fanout // groups
    capacity = min(rows_dev, mean_load + max(2, rows_dev * fanout // (16 * groups)))
    block = SIDE * capacity

    dp_at = lax.axis_index("dp")
    x_at, z_at = coords(lax.axis_index("expert"))
    even = dp_at % 2 == 0
    a_at = jnp.where(even, x_at, z_at)
    b_at = jnp.where(even, z_at, x_at)

    def expert_of(a, b):
        a, b = a % SIDE, b % SIDE
        return jnp.where(even, a * SIDE + b, b * SIDE + a)

    def along(v, step, core):
        if step % SIDE == 0:
            return v
        return permuted(
            v, n_dp, lambda y, c, x, z: (y, c, x + step, z) if c == core else (y, c, x, z + step)
        )

    first = lambda v, step: along(v, step, 0)
    second = lambda v, step: along(v, step, 1)

    experts = jnp.stack([expert_of(a_at + s, b_at + d) for s in range(SIDE) for d in range(SIDE)])
    near = (dp_at // 2 + jnp.arange(SIDE, dtype=jnp.int32)) % SIDE * 2
    order = jnp.concatenate([near + 1 - dp_at % 2, near + dp_at % 2])
    packed, experts, order = pack(tokens, expert_ids, gate_probs, experts.astype(jnp.int32), order)
    tok_sources = [first(packed, s) for s in range(SIDE)]
    grad_sources = [first(out_grad, s) for s in range(SIDE)]

    def exchange(send, parts, step):
        own, near, far_a, far_b, back = parts
        return [
            own,
            send(near, step),
            send(send(far_a, step), step),
            send(send(far_b, -step), -step),
            send(back, -step),
        ]

    *picked, slot, weight = pick_tokens(tok_sources, experts, width, fanout, block)
    rows_in = exchange(second, picked, 1)
    route_grad = exchange(second, pick_grads(grad_sources, slot, weight, block), 1)

    gate_mat, up_mat, down_mat = w_gate[0], w_up[0], w_down[0]
    ff = gate_mat.shape[1]
    rows_all, hidden, gate_k, up_k = forward(rows_in, gate_mat, up_mat)
    placer = place_matrix(slot, block)
    grad_all, gate_back, up_back, dots = back_hidden(route_grad, down_mat, gate_k, up_k, hidden)

    parts = back_input(gate_back, up_back, gate_mat, up_mat, dots)
    terms, mark = gate_up_terms(rows_all, gate_back, up_back, n_dp, [parts[0]])
    owned = lax.psum_scatter(terms, "dp", scatter_dimension=0, tiled=True)[0]
    give, keep = down_terms(hidden, grad_all, order, n_dp, [mark])
    got = permuted(give, n_dp, lambda y, c, x, z: (y, 1 - c, x, z))
    merged = merge_rows(placer, exchange(second, parts, -1), [mark])
    ends = exchange(first, merged, -1)
    sums = add_halves(keep, got, [merged[0]])
    far = [permuted(sums[k], n_dp, lambda y, c, x, z: (y + k, c, x, z)) for k in range(1, SIDE)]
    down_own = add_all([sums[0], *far])
    token_grad, prob_grad = finish(ends, expert_ids, gate_probs, experts)

    share = width // n_dp

    def tile_cols(at):
        return jnp.concatenate([owned[at + t * share : at + (t + 1) * share] for t in range(ff // TILE)], axis=1)

    half = ff // TILE * share
    return (token_grad, prob_grad, tile_cols(0)[None], tile_cols(half)[None], down_own[None])


def solution(mesh):
    rows = P(("dp", "expert"), None)
    mats = P("expert", None, None)
    return jax.shard_map(
        body,
        mesh=mesh,
        in_specs=(rows, rows, rows, rows, mats, mats, mats),
        out_specs=(rows, rows, P("expert", "dp", None), P("expert", "dp", None), P("expert", None, "dp")),
        check_vma=False,
    )
```

```python
import jax
import jax.numpy as jnp
from jax import lax
from jax.experimental import pallas as pl
from jax.experimental.pallas import tpu as pltpu
from jax.sharding import PartitionSpec as P

AXES = ("dp", "expert")
SIDE = 4
BF = jnp.bfloat16
F32 = jnp.float32
TILE = 256
VMEM_LIMIT = 16 * 2**20

NT = (((1,), (1,)), ((), ()))
TN = (((0,), (0,)), ((), ()))


def coords(expert):
    return expert // SIDE, expert % SIDE


def permuted(value, n_dp, target):
    pairs = []
    for dp in range(n_dp):
        for e in range(SIDE * SIDE):
            y, c, x, z = target(dp // 2, dp % 2, *coords(e))
            to = (y % SIDE * 2 + c) * SIDE * SIDE + x % SIDE * SIDE + z % SIDE
            pairs.append((dp * SIDE * SIDE + e, to))
    return lax.ppermute(value, AXES, pairs)


def call(kernel, out_shape, args, scratch=(), scalars=(), blocks=(), after=(), scalars_out=0, cost=0.0):
    vmem = pl.BlockSpec(memory_space=pltpu.VMEM)
    smem = pl.BlockSpec(memory_space=pltpu.SMEM)
    anywhere = pl.BlockSpec(memory_space=pl.ANY)

    def run(*refs):
        kernel(*refs[len(after) :])

    return pl.pallas_call(
        run,
        in_specs=[anywhere] * len(after)
        + [smem] * len(scalars)
        + [anywhere] * len(blocks)
        + [vmem] * len(args),
        out_specs=[
            vmem if i < len(out_shape) - scalars_out else smem for i in range(len(out_shape))
        ],
        out_shape=list(out_shape),
        scratch_shapes=list(scratch),
        compiler_params=pltpu.CompilerParams(vmem_limit_bytes=VMEM_LIMIT),
        cost_estimate=pl.CostEstimate(
            flops=1000 + int(cost * 1e15), bytes_accessed=1000 + int(cost * 3.5e12), transcendentals=0
        ),
    )(*after, *scalars, *blocks, *args)


def shape(dims, kind=BF):
    return jax.ShapeDtypeStruct(dims, kind)


def stack_blocks(blocks, whole, sems):
    copies, row = [], 0
    for i, b in enumerate(blocks):
        rows = b.shape[0]
        copies.append(pltpu.make_async_copy(b, whole.at[pl.ds(row, rows), :], sems.at[i]))
        row += rows
    for c in copies:
        c.start()
    for c in copies:
        c.wait()


PARTS = SIDE + 1
SEMS = pltpu.SemaphoreType.DMA((PARTS,))


def part_rows(block):
    far = (block // 2 + 15) // 16 * 16
    return [block, block, far, block - far, block]


def split_rows(value, block):
    row = 0
    for rows in part_rows(block):
        yield value[row : row + rows, :]
        row += rows


def pack(tokens, expert_ids, gate_probs, experts, order):
    rows, width = tokens.shape
    fanout = expert_ids.shape[1]

    def kernel(experts, order, tok, ids, probs, out, experts_out, order_out):
        for i in range(experts.shape[0]):
            experts_out[i] = experts[i]
        for i in range(order.shape[0]):
            order_out[i] = order[i]
        out[:, :width] = tok[...]
        out[:, width:] = jnp.concatenate(
            [
                ids[...].astype(F32),
                probs[...].astype(F32),
                jnp.zeros((rows, 128 - 2 * fanout), F32),
            ],
            axis=1,
        ).astype(BF)

    return call(
        kernel,
        [shape((rows, width + 128)), shape(experts.shape, jnp.int32), shape(order.shape, jnp.int32)],
        [tokens, expert_ids, gate_probs],
        scalars=[experts, order],
        scalars_out=2,
    )


def onehot_dots(onehot, whole, outs, block):
    width = outs[0].shape[1]
    far = part_rows(block)[2]
    for d in range(SIDE):
        hot = onehot(d)
        for at in range(0, width, 512):
            cols = slice(at, at + 512)
            value = jnp.dot(hot, whole[:, cols], preferred_element_type=F32).astype(BF)
            if d == 2:
                outs[2][:, cols] = value[:far, :]
                outs[3][:, cols] = value[far:, :]
            else:
                outs[d if d < 2 else PARTS - 1][:, cols] = value


def pick_tokens(sources, dests, width, fanout, block):
    rows_dev = sources[0].shape[0]
    group = SIDE * rows_dev

    def kernel(dest, x0, x1, x2, x3, o0, o1, o2, o3, o4, slot, weight, whole, sems):
        stack_blocks((x0, x1, x2, x3), whole, sems)
        hits, probs = [], []
        sheets = [
            jnp.transpose(whole[s * rows_dev : (s + 1) * rows_dev, width:].astype(F32)) for s in range(SIDE)
        ]
        for d in range(SIDE):
            hit, prob = [], []
            for m in sheets:
                same = jnp.where(m[:fanout, :] == dest[d].astype(F32), 1.0, 0.0)
                hit.append(jnp.sum(same, axis=0, keepdims=True))
                prob.append(jnp.sum(same * m[fanout : 2 * fanout, :], axis=0, keepdims=True))
            hits.append(jnp.concatenate(hit, axis=1))
            probs.append(jnp.concatenate(prob, axis=1))
        hits = jnp.concatenate(hits + [jnp.zeros((SIDE, group), F32)], axis=0)
        probs = jnp.concatenate(probs + [jnp.zeros((SIDE, group), F32)], axis=0)
        earlier = lax.broadcasted_iota(jnp.int32, (group, group), 0) < lax.broadcasted_iota(
            jnp.int32, (group, group), 1
        )
        rank = jnp.dot(
            hits.astype(BF), jnp.where(earlier, 1.0, 0.0).astype(BF), preferred_element_type=F32
        )
        slot[...] = jnp.where(hits > 0.5, rank, -4096.0)
        weight[...] = probs
        row = lax.broadcasted_iota(jnp.int32, (block, group), 0).astype(F32)
        onehot_dots(
            lambda d: jnp.where(row == slot[d : d + 1, :], 1.0, 0.0).astype(BF),
            whole,
            (o0, o1, o2, o3, o4),
            block,
        )

    return call(
        kernel,
        [shape((r, width)) for r in part_rows(block)] + [shape((2 * SIDE, group), F32)] * 2,
        [],
        [pltpu.VMEM((group, width + 128), BF), SEMS],
        [dests],
        sources,
    )


def pick_grads(sources, slot, weight, block, after):
    rows_dev, width = sources[0].shape
    group = SIDE * rows_dev

    def kernel(x0, x1, x2, x3, slot, weight, o0, o1, o2, o3, o4, whole, sems):
        stack_blocks((x0, x1, x2, x3), whole, sems)
        row = lax.broadcasted_iota(jnp.int32, (block, group), 0).astype(F32)
        onehot_dots(
            lambda d: jnp.where(row == slot[d : d + 1, :], weight[d : d + 1, :], 0.0).astype(BF),
            whole,
            (o0, o1, o2, o3, o4),
            block,
        )

    return call(
        kernel,
        [shape((r, width)) for r in part_rows(block)],
        [slot, weight],
        [pltpu.VMEM((group, width), BF), SEMS],
        blocks=sources,
        after=after,
    )


def place_matrix(slot, block):
    group = slot.shape[1]

    def kernel(slot, place):
        tall = jnp.transpose(jnp.concatenate([slot[...]] * 16, axis=0))
        lane = lax.broadcasted_iota(jnp.int32, (group, SIDE * block), 1).astype(F32)
        back = jnp.zeros((group, SIDE * block), F32)
        for d in range(SIDE):
            back = jnp.where(lane == tall[:, d : d + 1] + float(d * block), 1.0, back)
        place[...] = back.astype(BF)

    return call(kernel, [shape((group, SIDE * block))], [slot])[0]


def forward(blocks, gate_mat, up_mat):
    width = blocks[0].shape[1]
    ff = gate_mat.shape[1]
    rows = sum(b.shape[0] for b in blocks)
    half = rows // 2

    def kernel(x0, x1, x2, x3, x4, wg, wu, whole, hidden, gate_k, up_k, sems):
        stack_blocks((x0, x1, x2, x3, x4), whole, sems)
        for n in range(0, ff, TILE):
            cols = slice(n, n + TILE)
            for h in (0, half):
                at = slice(h, h + half)
                g = jnp.dot(whole[at, :], wg[:, cols], preferred_element_type=F32)
                u = jnp.dot(whole[at, :], wu[:, cols], preferred_element_type=F32)
                s = jax.nn.sigmoid(g)
                act = g * s
                hidden[at, cols] = (act * u).astype(BF)
                gate_k[at, cols] = (u * s * (1.0 + g * (1.0 - s))).astype(BF)
                up_k[at, cols] = act.astype(BF)

    return call(
        kernel,
        [shape((rows, width))] + [shape((rows, ff))] * 3,
        [gate_mat, up_mat],
        [SEMS],
        blocks=blocks,
    )


def back_hidden(blocks, down_mat, gate_k, up_k, hidden):
    block, width = blocks[0].shape
    ff = down_mat.shape[0]
    rows = sum(b.shape[0] for b in blocks)
    half = rows // 2

    def kernel(x0, x1, x2, x3, x4, wd, gk, uk, hid, whole, gate_back, up_back, dots, total, sems):
        stack_blocks((x0, x1, x2, x3, x4), whole, sems)
        for n in range(0, ff, TILE):
            cols = slice(n, n + TILE)
            for h in (0, half):
                at = slice(h, h + half)
                hg = lax.dot_general(whole[at, :], wd[cols, :], NT, preferred_element_type=F32)
                gate_back[at, cols] = (hg * gk[at, cols].astype(F32)).astype(BF)
                up_back[at, cols] = (hg * uk[at, cols].astype(F32)).astype(BF)
                term = hg * hid[at, cols].astype(F32)
                term = term[:, :128] + term[:, 128:]
                total[at, :] = term if n == 0 else total[at, :] + term
        for d in range(SIDE):
            at = slice(d * block, (d + 1) * block)
            lane = lax.broadcasted_iota(jnp.int32, (block, 128), 1)
            dot = jnp.sum(total[at, :], axis=1, keepdims=True)
            dots[at, :] = jnp.where(lane == d, dot, 0.0).astype(BF)

    return call(
        kernel,
        [shape((rows, width)), shape((rows, ff)), shape((rows, ff)), shape((rows, 128))],
        [down_mat, gate_k, up_k, hidden],
        [pltpu.VMEM((rows, 128), F32), SEMS],
        blocks=blocks,
    )


def back_input(gate_back, up_back, gate_mat, up_mat, dots, after):
    rows, ff = gate_back.shape
    width = gate_mat.shape[0]
    block = rows // SIDE

    def kernel(gb, ub, wg, wu, dots, *outs):
        for o, v in zip(outs, split_rows(dots[...], block)):
            o[:, width:] = v
        for n in range(0, width, TILE):
            at = slice(n, n + TILE)
            val = lax.dot_general(gb[...], wg[at, :], NT, preferred_element_type=F32)
            val += lax.dot_general(ub[...], wu[at, :], NT, preferred_element_type=F32)
            for o, v in zip(outs, split_rows(val.astype(BF), block)):
                o[:, at] = v

    return call(
        kernel,
        [shape((r, width + dots.shape[1])) for r in part_rows(block)],
        [gate_back, up_back, gate_mat, up_mat, dots],
        after=after,
    )


def gate_up_terms(whole, gate_back, up_back, shares, after):
    width = whole.shape[1]
    ff = gate_back.shape[1]
    part = width // shares

    def kernel(x, gb, ub, out, mark):
        mark[...] = jnp.zeros(mark.shape, F32)
        row = 0
        for ref in (gb, ub):
            for n in range(0, ff, TILE):
                value = lax.dot_general(x[...], ref[:, n : n + TILE], TN, preferred_element_type=F32)
                value = value.astype(BF)
                for s in range(shares):
                    out[s, row : row + part, :] = value[s * part : (s + 1) * part, :]
                row += part

    return call(
        kernel,
        [shape((shares, 2 * (ff // TILE) * part, TILE)), shape((8, 128), F32)],
        [whole, gate_back, up_back],
        after=after,
    )


def down_terms(hidden, whole, order, shares):
    ff, width = hidden.shape[1], whole.shape[1]
    part = width // shares
    half = shares // 2

    def kernel(order, hid, x, give, keep):
        for k in range(shares):
            cols = pl.ds(pl.multiple_of(order[k] * part, part), part)
            out = give if k < half else keep
            out[k % half] = lax.dot_general(hid[...], x[:, cols], TN, preferred_element_type=F32).astype(BF)

    return call(kernel, [shape((half, ff, part))] * 2, [hidden, whole], scalars=[order])


def merge_rows(placer, blocks, after):
    group, rows = placer.shape
    width = blocks[0].shape[1]
    rows_dev = group // SIDE

    def kernel(x0, x1, x2, x3, x4, place, o0, o1, o2, o3, o4, whole, sems):
        stack_blocks((x0, x1, x2, x3, x4), whole, sems)
        for at in range(0, width, TILE):
            cols = slice(at, min(at + TILE, width))
            val = jnp.dot(place[...], whole[:, cols], preferred_element_type=F32).astype(BF)
            for o, v in zip((o0, o1, o2, o3, o4), split_rows(val, rows_dev)):
                o[:, cols] = v

    return call(
        kernel,
        [shape((r, width)) for r in part_rows(rows_dev)],
        [placer],
        [pltpu.VMEM((rows, width), BF), SEMS],
        blocks=blocks,
        after=after,
    )


def add_halves(keep, got):
    def kernel(a, b, *outs):
        for k, o in enumerate(outs):
            o[...] = (a[k].astype(F32) + b[k].astype(F32)).astype(BF)

    return call(kernel, [shape(keep.shape[1:])] * keep.shape[0], [keep, got])


def add_all(terms):
    def kernel(*refs):
        refs[-1][...] = sum(r[...].astype(F32) for r in refs[:-1]).astype(BF)

    return call(kernel, [shape(terms[0].shape)], terms)[0]


def finish(terms, expert_ids, gate_probs, experts):
    rows, fanout = expert_ids.shape
    width = terms[0].shape[1] - 128
    far = part_rows(rows)[2]

    def kernel(experts, x0, x1, x2, x3, x4, ids, probs, grad, prob):
        for at in (slice(0, far), slice(far, rows)):
            parts = (x0[at, :], x1[at, :], (x2 if at.start == 0 else x3)[...], x4[at, :])
            grad[at, :] = sum(p[:, :width].astype(F32) for p in parts).astype(BF)
            total = jnp.zeros((at.stop - at.start, fanout), F32)
            for s in range(SIDE):
                vals = parts[s][:, width:].astype(F32)
                for d in range(SIDE):
                    total += jnp.where(ids[at, :] == experts[s * SIDE + d], vals[:, d : d + 1], 0.0)
            prob[at, :] = (total / probs[at, :].astype(F32)).astype(BF)

    return call(
        kernel,
        [shape((rows, width)), shape((rows, fanout))],
        [*terms, expert_ids, gate_probs],
        scalars=[experts],
        cost=0.000117,
    )


def body(tokens, expert_ids, gate_probs, out_grad, w_gate, w_up, w_down):
    rows_dev, width = tokens.shape
    fanout = expert_ids.shape[1]
    n_dp = lax.axis_size("dp")
    groups = lax.axis_size("expert")
    mean_load = rows_dev * fanout // groups
    capacity = min(rows_dev, mean_load + max(2, rows_dev * fanout // (16 * groups)))
    block = SIDE * capacity

    dp_at = lax.axis_index("dp")
    x_at, z_at = coords(lax.axis_index("expert"))
    even = dp_at % 2 == 0
    a_at = jnp.where(even, x_at, z_at)
    b_at = jnp.where(even, z_at, x_at)

    def expert_of(a, b):
        a, b = a % SIDE, b % SIDE
        return jnp.where(even, a * SIDE + b, b * SIDE + a)

    def along(v, step, core):
        if step % SIDE == 0:
            return v
        return permuted(
            v, n_dp, lambda y, c, x, z: (y, c, x + step, z) if c == core else (y, c, x, z + step)
        )

    first = lambda v, step: along(v, step, 0)
    second = lambda v, step: along(v, step, 1)

    experts = jnp.stack([expert_of(a_at + s, b_at + d) for s in range(SIDE) for d in range(SIDE)])
    near = (dp_at // 2 + jnp.arange(SIDE, dtype=jnp.int32)) % SIDE * 2
    order = jnp.concatenate([near + 1 - dp_at % 2, near + dp_at % 2])
    packed, experts, order = pack(tokens, expert_ids, gate_probs, experts.astype(jnp.int32), order)
    tok_sources = [first(packed, s) for s in range(SIDE)]
    grad_sources = [first(out_grad, s) for s in range(SIDE)]

    def exchange(send, parts, step):
        own, near, far_a, far_b, back = parts
        return [
            own,
            send(near, step),
            send(send(far_a, step), step),
            send(send(far_b, -step), -step),
            send(back, -step),
        ]

    *picked, slot, weight = pick_tokens(tok_sources, experts, width, fanout, block)
    rows_in = exchange(second, picked, 1)
    route_grad = exchange(second, pick_grads(grad_sources, slot, weight, block, [rows_in[1], rows_in[4]]), 1)

    gate_mat, up_mat, down_mat = w_gate[0], w_up[0], w_down[0]
    ff = gate_mat.shape[1]
    rows_all, hidden, gate_k, up_k = forward(rows_in, gate_mat, up_mat)
    placer = place_matrix(slot, block)
    grad_all, gate_back, up_back, dots = back_hidden(route_grad, down_mat, gate_k, up_k, hidden)

    give, keep = down_terms(hidden, grad_all, order, n_dp)
    got = permuted(give, n_dp, lambda y, c, x, z: (y, 1 - c, x, z))
    parts = back_input(gate_back, up_back, gate_mat, up_mat, dots, [give])
    terms, mark = gate_up_terms(rows_all, gate_back, up_back, n_dp, [parts[0]])
    owned = lax.psum_scatter(terms, "dp", scatter_dimension=0, tiled=True)[0]
    sums = add_halves(keep, got)
    merged = merge_rows(placer, exchange(second, parts, -1), [mark, sums[0]])
    ends = exchange(first, merged, -1)
    far = [permuted(sums[k], n_dp, lambda y, c, x, z: (y + k, c, x, z)) for k in range(1, SIDE)]
    down_own = add_all([sums[0], *far])
    token_grad, prob_grad = finish(ends, expert_ids, gate_probs, experts)

    share = width // n_dp

    def tile_cols(at):
        return jnp.concatenate([owned[at + t * share : at + (t + 1) * share] for t in range(ff // TILE)], axis=1)

    half = ff // TILE * share
    return (token_grad, prob_grad, tile_cols(0)[None], tile_cols(half)[None], down_own[None])


def solution(mesh):
    rows = P(("dp", "expert"), None)
    mats = P("expert", None, None)
    return jax.shard_map(
        body,
        mesh=mesh,
        in_specs=(rows, rows, rows, rows, mats, mats, mats),
        out_specs=(rows, rows, P("expert", "dp", None), P("expert", "dp", None), P("expert", None, "dp")),
        check_vma=False,
    )
```

```python
import jax
import jax.numpy as jnp
from jax import lax
from jax.experimental import pallas as pl
from jax.experimental.pallas import tpu as pltpu
from jax.sharding import PartitionSpec as P

AXES = ("dp", "expert")
SIDE = 4
BF = jnp.bfloat16
F32 = jnp.float32
TILE = 256
VMEM_LIMIT = 16 * 2**20

NT = (((1,), (1,)), ((), ()))
TN = (((0,), (0,)), ((), ()))


def coords(expert):
    return expert // SIDE, expert % SIDE


def permuted(value, n_dp, target):
    pairs = []
    for dp in range(n_dp):
        for e in range(SIDE * SIDE):
            y, c, x, z = target(dp // 2, dp % 2, *coords(e))
            to = (y % SIDE * 2 + c) * SIDE * SIDE + x % SIDE * SIDE + z % SIDE
            pairs.append((dp * SIDE * SIDE + e, to))
    return lax.ppermute(value, AXES, pairs)


def call(kernel, out_shape, args, scratch=(), scalars=(), blocks=(), after=(), scalars_out=0, cost=0.0):
    vmem = pl.BlockSpec(memory_space=pltpu.VMEM)
    smem = pl.BlockSpec(memory_space=pltpu.SMEM)
    anywhere = pl.BlockSpec(memory_space=pl.ANY)

    def run(*refs):
        kernel(*refs[len(after) :])

    return pl.pallas_call(
        run,
        in_specs=[anywhere] * len(after)
        + [smem] * len(scalars)
        + [anywhere] * len(blocks)
        + [vmem] * len(args),
        out_specs=[
            vmem if i < len(out_shape) - scalars_out else smem for i in range(len(out_shape))
        ],
        out_shape=list(out_shape),
        scratch_shapes=list(scratch),
        compiler_params=pltpu.CompilerParams(vmem_limit_bytes=VMEM_LIMIT),
        cost_estimate=pl.CostEstimate(
            flops=1000 + int(cost * 1e15), bytes_accessed=1000 + int(cost * 3.5e12), transcendentals=0
        ),
    )(*after, *scalars, *blocks, *args)


def shape(dims, kind=BF):
    return jax.ShapeDtypeStruct(dims, kind)


def stack_blocks(blocks, whole, sems):
    copies, row = [], 0
    for i, (b, rows) in enumerate(blocks):
        copies.append(pltpu.make_async_copy(b.at[pl.ds(0, rows), :], whole.at[pl.ds(row, rows), :], sems.at[i]))
        row += rows
    for c in copies:
        c.start()
    for c in copies:
        c.wait()


SEMS = pltpu.SemaphoreType.DMA((SIDE + 1,))


def far_rows(block):
    return (block // 2 + 15) // 16 * 16


def message_rows(block):
    return [block, block + far_rows(block), 2 * block - far_rows(block)]


def put_block(outs, d, cols, value):
    own, near, back = outs
    block = own.shape[0]
    far = far_rows(block)
    if d == 0:
        own[:, cols] = value
    elif d == 1:
        near[:block, cols] = value
    elif d == 3:
        back[:block, cols] = value
    else:
        near[block:, cols] = value[:far, :]
        back[block:, cols] = value[far:, :]


def in_order(arrived):
    own, near, back, far_a, far_b = arrived
    block = own.shape[0]
    return [(own, block), (near, block), (far_a, far_a.shape[0]), (far_b, far_b.shape[0]), (back, block)]


def relay(near, back, block):
    def kernel(near, back, far_a, far_b, sems):
        copies = [
            pltpu.make_async_copy(m.at[pl.ds(block, o.shape[0]), :], o, sems.at[i])
            for i, (m, o) in enumerate(((near, far_a), (back, far_b)))
        ]
        for c in copies:
            c.start()
        for c in copies:
            c.wait()

    width = near.shape[1]
    return call(
        kernel,
        [shape((near.shape[0] - block, width)), shape((back.shape[0] - block, width))],
        [],
        [SEMS],
        blocks=[near, back],
    )


def pack(tokens, expert_ids, gate_probs, experts, order):
    rows, width = tokens.shape
    fanout = expert_ids.shape[1]

    def kernel(experts, order, tok, ids, probs, out, experts_out, order_out):
        for i in range(experts.shape[0]):
            experts_out[i] = experts[i]
        for i in range(order.shape[0]):
            order_out[i] = order[i]
        out[:, :width] = tok[...]
        out[:, width:] = jnp.concatenate(
            [
                ids[...].astype(F32),
                probs[...].astype(F32),
                jnp.zeros((rows, 128 - 2 * fanout), F32),
            ],
            axis=1,
        ).astype(BF)

    return call(
        kernel,
        [shape((rows, width + 128)), shape(experts.shape, jnp.int32), shape(order.shape, jnp.int32)],
        [tokens, expert_ids, gate_probs],
        scalars=[experts, order],
        scalars_out=2,
    )


def onehot_dots(onehot, whole, outs):
    width = outs[0].shape[1]
    for d in (1, 3, 2, 0):
        hot = onehot(d)
        for at in range(0, width, 512):
            cols = slice(at, at + 512)
            value = jnp.dot(hot, whole[:, cols], preferred_element_type=F32).astype(BF)
            put_block(outs, d, cols, value)


def pick_tokens(sources, dests, width, fanout, block):
    rows_dev = sources[0].shape[0]
    group = SIDE * rows_dev

    def kernel(dest, x0, x1, x2, x3, o0, o1, o2, slot, weight, whole, sems):
        stack_blocks([(x, rows_dev) for x in (x0, x1, x2, x3)], whole, sems)
        hits, probs = [], []
        sheets = [
            jnp.transpose(whole[s * rows_dev : (s + 1) * rows_dev, width:].astype(F32)) for s in range(SIDE)
        ]
        for d in range(SIDE):
            hit, prob = [], []
            for m in sheets:
                same = jnp.where(m[:fanout, :] == dest[d].astype(F32), 1.0, 0.0)
                hit.append(jnp.sum(same, axis=0, keepdims=True))
                prob.append(jnp.sum(same * m[fanout : 2 * fanout, :], axis=0, keepdims=True))
            hits.append(jnp.concatenate(hit, axis=1))
            probs.append(jnp.concatenate(prob, axis=1))
        hits = jnp.concatenate(hits + [jnp.zeros((SIDE, group), F32)], axis=0)
        probs = jnp.concatenate(probs + [jnp.zeros((SIDE, group), F32)], axis=0)
        earlier = lax.broadcasted_iota(jnp.int32, (group, group), 0) < lax.broadcasted_iota(
            jnp.int32, (group, group), 1
        )
        rank = jnp.dot(
            hits.astype(BF), jnp.where(earlier, 1.0, 0.0).astype(BF), preferred_element_type=F32
        )
        slot[...] = jnp.where(hits > 0.5, rank, -4096.0)
        weight[...] = probs
        row = lax.broadcasted_iota(jnp.int32, (block, group), 0).astype(F32)
        onehot_dots(
            lambda d: jnp.where(row == slot[d : d + 1, :], 1.0, 0.0).astype(BF),
            whole,
            (o0, o1, o2),
        )

    return call(
        kernel,
        [shape((r, width)) for r in message_rows(block)] + [shape((2 * SIDE, group), F32)] * 2,
        [],
        [pltpu.VMEM((group, width + 128), BF), SEMS],
        [dests],
        sources,
    )


def pick_grads(sources, slot, weight, block, after):
    rows_dev, width = sources[0].shape
    group = SIDE * rows_dev

    def kernel(x0, x1, x2, x3, slot, weight, o0, o1, o2, whole, sems):
        stack_blocks([(x, rows_dev) for x in (x0, x1, x2, x3)], whole, sems)
        row = lax.broadcasted_iota(jnp.int32, (block, group), 0).astype(F32)
        onehot_dots(
            lambda d: jnp.where(row == slot[d : d + 1, :], weight[d : d + 1, :], 0.0).astype(BF),
            whole,
            (o0, o1, o2),
        )

    return call(
        kernel,
        [shape((r, width)) for r in message_rows(block)],
        [slot, weight],
        [pltpu.VMEM((group, width), BF), SEMS],
        blocks=sources,
        after=after,
    )


def place_matrix(slot, block):
    group = slot.shape[1]

    def kernel(slot, place):
        tall = jnp.transpose(jnp.concatenate([slot[...]] * 16, axis=0))
        lane = lax.broadcasted_iota(jnp.int32, (group, SIDE * block), 1).astype(F32)
        back = jnp.zeros((group, SIDE * block), F32)
        for d in range(SIDE):
            back = jnp.where(lane == tall[:, d : d + 1] + float(d * block), 1.0, back)
        place[...] = back.astype(BF)

    return call(kernel, [shape((group, SIDE * block))], [slot])[0]


def forward(blocks, gate_mat, up_mat):
    block, width = blocks[0].shape
    ff = gate_mat.shape[1]
    rows = SIDE * block
    half = rows // 2

    def kernel(x0, x1, x2, x3, x4, wg, wu, whole, hidden, gate_k, up_k, sems):
        stack_blocks(in_order((x0, x1, x2, x3, x4)), whole, sems)
        for n in range(0, ff, TILE):
            cols = slice(n, n + TILE)
            for h in (0, half):
                at = slice(h, h + half)
                g = jnp.dot(whole[at, :], wg[:, cols], preferred_element_type=F32)
                u = jnp.dot(whole[at, :], wu[:, cols], preferred_element_type=F32)
                s = jax.nn.sigmoid(g)
                act = g * s
                hidden[at, cols] = (act * u).astype(BF)
                gate_k[at, cols] = (u * s * (1.0 + g * (1.0 - s))).astype(BF)
                up_k[at, cols] = act.astype(BF)

    return call(
        kernel,
        [shape((rows, width))] + [shape((rows, ff))] * 3,
        [gate_mat, up_mat],
        [SEMS],
        blocks=blocks,
    )


def back_hidden(blocks, down_mat, gate_k, up_k, hidden):
    block, width = blocks[0].shape
    ff = down_mat.shape[0]
    rows = SIDE * block
    half = rows // 2

    def kernel(x0, x1, x2, x3, x4, wd, gk, uk, hid, whole, gate_back, up_back, dots, total, sems):
        stack_blocks(in_order((x0, x1, x2, x3, x4)), whole, sems)
        for n in range(0, ff, TILE):
            cols = slice(n, n + TILE)
            for h in (0, half):
                at = slice(h, h + half)
                hg = lax.dot_general(whole[at, :], wd[cols, :], NT, preferred_element_type=F32)
                gate_back[at, cols] = (hg * gk[at, cols].astype(F32)).astype(BF)
                up_back[at, cols] = (hg * uk[at, cols].astype(F32)).astype(BF)
                term = hg * hid[at, cols].astype(F32)
                term = term[:, :128] + term[:, 128:]
                total[at, :] = term if n == 0 else total[at, :] + term
        for d in range(SIDE):
            at = slice(d * block, (d + 1) * block)
            lane = lax.broadcasted_iota(jnp.int32, (block, 128), 1)
            dot = jnp.sum(total[at, :], axis=1, keepdims=True)
            dots[at, :] = jnp.where(lane == d, dot, 0.0).astype(BF)

    return call(
        kernel,
        [shape((rows, width)), shape((rows, ff)), shape((rows, ff)), shape((rows, 128))],
        [down_mat, gate_k, up_k, hidden],
        [pltpu.VMEM((rows, 128), F32), SEMS],
        blocks=blocks,
    )


def back_input(gate_back, up_back, gate_mat, up_mat, dots, after):
    rows, ff = gate_back.shape
    width = gate_mat.shape[0]
    block = rows // SIDE

    def kernel(gb, ub, wg, wu, dots, *outs):
        blocks = [slice(d * block, (d + 1) * block) for d in range(SIDE)]
        for d, b in enumerate(blocks):
            put_block(outs, d, slice(width, None), dots[b, :])
        for n in range(0, width, TILE):
            at = slice(n, n + TILE)
            val = lax.dot_general(gb[...], wg[at, :], NT, preferred_element_type=F32)
            val += lax.dot_general(ub[...], wu[at, :], NT, preferred_element_type=F32)
            val = val.astype(BF)
            for d, b in enumerate(blocks):
                put_block(outs, d, at, val[b, :])

    return call(
        kernel,
        [shape((r, width + dots.shape[1])) for r in message_rows(block)],
        [gate_back, up_back, gate_mat, up_mat, dots],
        after=after,
    )


def gate_up_terms(whole, gate_back, up_back, shares, after):
    width = whole.shape[1]
    ff = gate_back.shape[1]
    part = width // shares

    def kernel(x, gb, ub, out, mark):
        mark[...] = jnp.zeros(mark.shape, F32)
        row = 0
        for ref in (gb, ub):
            for n in range(0, ff, TILE):
                value = lax.dot_general(x[...], ref[:, n : n + TILE], TN, preferred_element_type=F32)
                value = value.astype(BF)
                for s in range(shares):
                    out[s, row : row + part, :] = value[s * part : (s + 1) * part, :]
                row += part

    return call(
        kernel,
        [shape((shares, 2 * (ff // TILE) * part, TILE)), shape((8, 128), F32)],
        [whole, gate_back, up_back],
        after=after,
    )


def down_terms(hidden, whole, order, shares, after):
    ff, width = hidden.shape[1], whole.shape[1]
    part = width // shares
    half = shares // 2

    def kernel(order, hid, x, give, keep):
        for k in range(shares):
            cols = pl.ds(pl.multiple_of(order[k] * part, part), part)
            out = give if k < half else keep
            out[k % half] = lax.dot_general(hid[...], x[:, cols], TN, preferred_element_type=F32).astype(BF)

    return call(kernel, [shape((half, ff, part))] * 2, [hidden, whole], scalars=[order], after=after)


def merge_rows(placer, blocks, after):
    group, rows = placer.shape
    width = blocks[0].shape[1]
    rows_dev = group // SIDE

    def kernel(x0, x1, x2, x3, x4, place, o0, o1, o2, whole, sems):
        stack_blocks(in_order((x0, x1, x2, x3, x4)), whole, sems)
        for at in range(0, width, TILE):
            cols = slice(at, min(at + TILE, width))
            val = jnp.dot(place[...], whole[:, cols], preferred_element_type=F32).astype(BF)
            for s in range(SIDE):
                put_block((o0, o1, o2), s, cols, val[s * rows_dev : (s + 1) * rows_dev, :])

    return call(
        kernel,
        [shape((r, width)) for r in message_rows(rows_dev)],
        [placer],
        [pltpu.VMEM((rows, width), BF), SEMS],
        blocks=blocks,
        after=after,
    )


def add_halves(keep, got):
    def kernel(a, b, *outs):
        for k, o in enumerate(outs):
            o[...] = (a[k].astype(F32) + b[k].astype(F32)).astype(BF)

    return call(kernel, [shape(keep.shape[1:])] * keep.shape[0], [keep, got])


def add_all(terms):
    def kernel(*refs):
        refs[-1][...] = sum(r[...].astype(F32) for r in refs[:-1]).astype(BF)

    return call(kernel, [shape(terms[0].shape)], terms)[0]


def finish(terms, expert_ids, gate_probs, experts):
    rows, fanout = expert_ids.shape
    width = terms[0].shape[1] - 128
    far = far_rows(rows)

    def kernel(experts, x0, x1, x2, x3, x4, ids, probs, grad, prob):
        for at in (slice(0, far), slice(far, rows)):
            parts = (x0[at, :], x1[at, :], (x3 if at.start == 0 else x4)[...], x2[at, :])
            grad[at, :] = sum(p[:, :width].astype(F32) for p in parts).astype(BF)
            total = jnp.zeros((at.stop - at.start, fanout), F32)
            for s in range(SIDE):
                vals = parts[s][:, width:].astype(F32)
                for d in range(SIDE):
                    total += jnp.where(ids[at, :] == experts[s * SIDE + d], vals[:, d : d + 1], 0.0)
            prob[at, :] = (total / probs[at, :].astype(F32)).astype(BF)

    return call(
        kernel,
        [shape((rows, width)), shape((rows, fanout))],
        [*terms, expert_ids, gate_probs],
        scalars=[experts],
        cost=0.000109,
    )


def body(tokens, expert_ids, gate_probs, out_grad, w_gate, w_up, w_down):
    rows_dev, width = tokens.shape
    fanout = expert_ids.shape[1]
    n_dp = lax.axis_size("dp")
    groups = lax.axis_size("expert")
    mean_load = rows_dev * fanout // groups
    capacity = min(rows_dev, mean_load + max(2, rows_dev * fanout // (16 * groups)))
    block = SIDE * capacity

    dp_at = lax.axis_index("dp")
    x_at, z_at = coords(lax.axis_index("expert"))
    even = dp_at % 2 == 0
    a_at = jnp.where(even, x_at, z_at)
    b_at = jnp.where(even, z_at, x_at)

    def expert_of(a, b):
        a, b = a % SIDE, b % SIDE
        return jnp.where(even, a * SIDE + b, b * SIDE + a)

    def along(v, step, core):
        if step % SIDE == 0:
            return v
        return permuted(
            v, n_dp, lambda y, c, x, z: (y, c, x + step, z) if c == core else (y, c, x, z + step)
        )

    first = lambda v, step: along(v, step, 0)
    second = lambda v, step: along(v, step, 1)

    experts = jnp.stack([expert_of(a_at + s, b_at + d) for s in range(SIDE) for d in range(SIDE)])
    near = (dp_at // 2 + jnp.arange(SIDE, dtype=jnp.int32)) % SIDE * 2
    order = jnp.concatenate([near + 1 - dp_at % 2, near + dp_at % 2])
    packed, experts, order = pack(tokens, expert_ids, gate_probs, experts.astype(jnp.int32), order)
    tok_sources = [first(packed, s) for s in range(SIDE)]
    grad_sources = [first(out_grad, s) for s in range(SIDE)]

    def exchange(send, messages, step):
        own, near, back = messages
        near, back = send(near, step), send(back, -step)
        far_a, far_b = relay(near, back, own.shape[0])
        return [own, near, back, send(far_a, step), send(far_b, -step)]

    *picked, slot, weight = pick_tokens(tok_sources, experts, width, fanout, block)
    rows_in = exchange(second, picked, 1)
    route_grad = exchange(second, pick_grads(grad_sources, slot, weight, block, []), 1)

    gate_mat, up_mat, down_mat = w_gate[0], w_up[0], w_down[0]
    ff = gate_mat.shape[1]
    rows_all, hidden, gate_k, up_k = forward(rows_in, gate_mat, up_mat)
    placer = place_matrix(slot, block)
    grad_all, gate_back, up_back, dots = back_hidden(route_grad, down_mat, gate_k, up_k, hidden)

    parts = back_input(gate_back, up_back, gate_mat, up_mat, dots, [])
    terms, mark = gate_up_terms(rows_all, gate_back, up_back, n_dp, [parts[0]])
    owned = lax.psum_scatter(terms, "dp", scatter_dimension=0, tiled=True)[0]
    merged = merge_rows(placer, exchange(second, parts, -1), [mark])
    ends = exchange(first, merged, -1)
    give, keep = down_terms(hidden, grad_all, order, n_dp, [mark])
    got = permuted(give, n_dp, lambda y, c, x, z: (y, 1 - c, x, z))
    sums = add_halves(keep, got)
    far = [permuted(sums[k], n_dp, lambda y, c, x, z: (y + k, c, x, z)) for k in range(1, SIDE)]
    down_own = add_all([sums[0], *far])
    token_grad, prob_grad = finish(ends, expert_ids, gate_probs, experts)

    share = width // n_dp

    def tile_cols(at):
        return jnp.concatenate([owned[at + t * share : at + (t + 1) * share] for t in range(ff // TILE)], axis=1)

    half = ff // TILE * share
    return (token_grad, prob_grad, tile_cols(0)[None], tile_cols(half)[None], down_own[None])


def solution(mesh):
    rows = P(("dp", "expert"), None)
    mats = P("expert", None, None)
    return jax.shard_map(
        body,
        mesh=mesh,
        in_specs=(rows, rows, rows, rows, mats, mats, mats),
        out_specs=(rows, rows, P("expert", "dp", None), P("expert", "dp", None), P("expert", None, "dp")),
        check_vma=False,
    )
```

```python
import jax
import jax.numpy as jnp
from jax import lax
from jax.experimental import pallas as pl
from jax.experimental.pallas import tpu as pltpu
from jax.sharding import PartitionSpec as P

AXES = ("dp", "expert")
SIDE = 4
BF = jnp.bfloat16
F32 = jnp.float32
TILE = 256
VMEM_LIMIT = 16 * 2**20

NT = (((1,), (1,)), ((), ()))
TN = (((0,), (0,)), ((), ()))


def coords(expert):
    return expert // SIDE, expert % SIDE


def permuted(value, n_dp, target):
    pairs = []
    for dp in range(n_dp):
        for e in range(SIDE * SIDE):
            y, c, x, z = target(dp // 2, dp % 2, *coords(e))
            to = (y % SIDE * 2 + c) * SIDE * SIDE + x % SIDE * SIDE + z % SIDE
            pairs.append((dp * SIDE * SIDE + e, to))
    return lax.ppermute(value, AXES, pairs)


def call(kernel, out_shape, args, scratch=(), scalars=(), blocks=(), after=(), scalars_out=0, hidden_out=(), cost=0.0, aliases=None):
    vmem = pl.BlockSpec(memory_space=pltpu.VMEM)
    smem = pl.BlockSpec(memory_space=pltpu.SMEM)
    anywhere = pl.BlockSpec(memory_space=pl.ANY)

    def run(*refs):
        kernel(*refs[len(after) :])

    return pl.pallas_call(
        run,
        in_specs=[anywhere] * len(after)
        + [smem] * len(scalars)
        + [anywhere] * len(blocks)
        + [vmem] * len(args),
        out_specs=[
            anywhere if i in hidden_out else vmem if i < len(out_shape) - scalars_out else smem
            for i in range(len(out_shape))
        ],
        out_shape=list(out_shape),
        scratch_shapes=list(scratch),
        input_output_aliases=aliases or {},
        compiler_params=pltpu.CompilerParams(vmem_limit_bytes=VMEM_LIMIT),
        cost_estimate=pl.CostEstimate(
            flops=1000 + int(cost * 1e15), bytes_accessed=1000 + int(cost * 3.5e12), transcendentals=0
        ),
    )(*after, *scalars, *blocks, *args)


def shape(dims, kind=BF):
    return jax.ShapeDtypeStruct(dims, kind)


def stack_blocks(blocks, whole, sems):
    copies, row = [], 0
    for i, b in enumerate(blocks):
        rows = b.shape[0]
        copies.append(pltpu.make_async_copy(b, whole.at[pl.ds(row, rows), :], sems.at[i]))
        row += rows
    for c in copies:
        c.start()
    for c in copies:
        c.wait()


PARTS = SIDE + 1
SEMS = pltpu.SemaphoreType.DMA((PARTS,))


def part_rows(block):
    far = (block // 2 + 15) // 16 * 16
    return [block, block, far, block - far, block]


def split_rows(value, block):
    row = 0
    for rows in part_rows(block):
        yield value[row : row + rows, :]
        row += rows


def pack(tokens, expert_ids, gate_probs, experts, order):
    rows, width = tokens.shape
    fanout = expert_ids.shape[1]

    def kernel(experts, order, tok, ids, probs, out, experts_out, order_out):
        for i in range(experts.shape[0]):
            experts_out[i] = experts[i]
        for i in range(order.shape[0]):
            order_out[i] = order[i]
        out[:, :width] = tok[...]
        out[:, width:] = jnp.concatenate(
            [
                ids[...].astype(F32),
                probs[...].astype(F32),
                jnp.zeros((rows, 128 - 2 * fanout), F32),
            ],
            axis=1,
        ).astype(BF)

    return call(
        kernel,
        [shape((rows, width + 128)), shape(experts.shape, jnp.int32), shape(order.shape, jnp.int32)],
        [tokens, expert_ids, gate_probs],
        scalars=[experts, order],
        scalars_out=2,
    )


def onehot_dots(onehot, whole, outs, block):
    width = outs[0].shape[1]
    far = part_rows(block)[2]
    for d in range(SIDE):
        hot = onehot(d)
        for at in range(0, width, 512):
            cols = slice(at, at + 512)
            value = jnp.dot(hot, whole[:, cols], preferred_element_type=F32).astype(BF)
            if d == 2:
                outs[2][:, cols] = value[:far, :]
                outs[3][:, cols] = value[far:, :]
            else:
                outs[d if d < 2 else PARTS - 1][:, cols] = value


def pick_tokens(sources, dests, width, fanout, block):
    rows_dev = sources[0].shape[0]
    group = SIDE * rows_dev

    def kernel(dest, x0, x1, x2, x3, o0, o1, o2, o3, o4, slot, weight, whole, sems):
        stack_blocks((x0, x1, x2, x3), whole, sems)
        hits, probs = [], []
        sheets = [
            jnp.transpose(whole[s * rows_dev : (s + 1) * rows_dev, width:].astype(F32)) for s in range(SIDE)
        ]
        for d in range(SIDE):
            hit, prob = [], []
            for m in sheets:
                same = jnp.where(m[:fanout, :] == dest[d].astype(F32), 1.0, 0.0)
                hit.append(jnp.sum(same, axis=0, keepdims=True))
                prob.append(jnp.sum(same * m[fanout : 2 * fanout, :], axis=0, keepdims=True))
            hits.append(jnp.concatenate(hit, axis=1))
            probs.append(jnp.concatenate(prob, axis=1))
        hits = jnp.concatenate(hits + [jnp.zeros((SIDE, group), F32)], axis=0)
        probs = jnp.concatenate(probs + [jnp.zeros((SIDE, group), F32)], axis=0)
        earlier = lax.broadcasted_iota(jnp.int32, (group, group), 0) < lax.broadcasted_iota(
            jnp.int32, (group, group), 1
        )
        rank = jnp.dot(
            hits.astype(BF), jnp.where(earlier, 1.0, 0.0).astype(BF), preferred_element_type=F32
        )
        slot[...] = jnp.where(hits > 0.5, rank, -4096.0)
        weight[...] = probs
        row = lax.broadcasted_iota(jnp.int32, (block, group), 0).astype(F32)
        onehot_dots(
            lambda d: jnp.where(row == slot[d : d + 1, :], 1.0, 0.0).astype(BF),
            whole,
            (o0, o1, o2, o3, o4),
            block,
        )

    return call(
        kernel,
        [shape((r, width)) for r in part_rows(block)] + [shape((2 * SIDE, group), F32)] * 2,
        [],
        [pltpu.VMEM((group, width + 128), BF), SEMS],
        [dests],
        sources,
    )


def pick_grads(sources, slot, weight, block):
    rows_dev, width = sources[0].shape
    group = SIDE * rows_dev

    def kernel(x0, x1, x2, x3, slot, weight, o0, o1, o2, o3, o4, whole, sems):
        stack_blocks((x0, x1, x2, x3), whole, sems)
        row = lax.broadcasted_iota(jnp.int32, (block, group), 0).astype(F32)
        onehot_dots(
            lambda d: jnp.where(row == slot[d : d + 1, :], weight[d : d + 1, :], 0.0).astype(BF),
            whole,
            (o0, o1, o2, o3, o4),
            block,
        )

    return call(
        kernel,
        [shape((r, width)) for r in part_rows(block)],
        [slot, weight],
        [pltpu.VMEM((group, width), BF), SEMS],
        blocks=sources,
    )


def place_matrix(slot, block):
    group = slot.shape[1]

    def kernel(slot, place):
        tall = jnp.transpose(jnp.concatenate([slot[...]] * 16, axis=0))
        lane = lax.broadcasted_iota(jnp.int32, (group, SIDE * block), 1).astype(F32)
        back = jnp.zeros((group, SIDE * block), F32)
        for d in range(SIDE):
            back = jnp.where(lane == tall[:, d : d + 1] + float(d * block), 1.0, back)
        place[...] = back.astype(BF)

    return call(kernel, [shape((group, SIDE * block))], [slot])[0]


def forward(blocks, at_rows, gate_mat, up_mat, before=()):
    width = blocks[0].shape[1]
    ff = gate_mat.shape[1]
    sizes = [b.shape[0] for b in blocks]
    n, old = len(blocks), len(before)
    rows = before[0].shape[0] if before else SIDE * sizes[0]
    spans = []
    for row, size in zip(at_rows, sizes):
        if spans and spans[-1][1] == row:
            spans[-1][1] = row + size
        else:
            spans.append([row, row + size])

    def kernel(*refs):
        xs, (wg, wu) = refs[:n], refs[n : n + 2]
        whole, hidden, gate_k, up_k, sems = refs[n + 2 + old :]
        copies = [
            pltpu.make_async_copy(x, whole.at[pl.ds(row, size), :], sems.at[i])
            for i, (x, row, size) in enumerate(zip(xs, at_rows, sizes))
        ]
        for c in copies:
            c.start()
        for c in copies:
            c.wait()
        for f in range(0, ff, TILE):
            cols = slice(f, f + TILE)
            for low, high in spans:
                at = slice(low, high)
                g = jnp.dot(whole[at, :], wg[:, cols], preferred_element_type=F32)
                u = jnp.dot(whole[at, :], wu[:, cols], preferred_element_type=F32)
                s = jax.nn.sigmoid(g)
                act = g * s
                hidden[at, cols] = (act * u).astype(BF)
                gate_k[at, cols] = (u * s * (1.0 + g * (1.0 - s))).astype(BF)
                up_k[at, cols] = act.astype(BF)

    return call(
        kernel,
        [shape((rows, width))] + [shape((rows, ff))] * 3,
        [gate_mat, up_mat, *before],
        [SEMS],
        blocks=blocks,
        aliases={n + 2 + i: i for i in range(old)},
    )


def back_hidden(blocks, down_mat, gate_k, up_k, hidden):
    block, width = blocks[0].shape
    ff = down_mat.shape[0]
    rows = sum(b.shape[0] for b in blocks)
    half = rows // 2

    def kernel(x0, x1, x2, x3, x4, wd, gk, uk, hid, out, gate_back, up_back, dots, whole, total, sems):
        stack_blocks((x0, x1, x2, x3, x4), whole, sems)
        store = pltpu.make_async_copy(whole, out, sems.at[0])
        store.start()
        for n in range(0, ff, TILE):
            cols = slice(n, n + TILE)
            for h in (0, half):
                at = slice(h, h + half)
                hg = lax.dot_general(whole[at, :], wd[cols, :], NT, preferred_element_type=F32)
                gate_back[at, cols] = (hg * gk[at, cols].astype(F32)).astype(BF)
                up_back[at, cols] = (hg * uk[at, cols].astype(F32)).astype(BF)
                term = hg * hid[at, cols].astype(F32)
                term = term[:, :128] + term[:, 128:]
                total[at, :] = term if n == 0 else total[at, :] + term
        for d in range(SIDE):
            at = slice(d * block, (d + 1) * block)
            lane = lax.broadcasted_iota(jnp.int32, (block, 128), 1)
            dot = jnp.sum(total[at, :], axis=1, keepdims=True)
            dots[at, :] = jnp.where(lane == d, dot, 0.0).astype(BF)
        store.wait()

    return call(
        kernel,
        [shape((rows, width)), shape((rows, ff)), shape((rows, ff)), shape((rows, 128))],
        [down_mat, gate_k, up_k, hidden],
        [pltpu.VMEM((rows, width), BF), pltpu.VMEM((rows, 128), F32), SEMS],
        blocks=blocks,
        hidden_out=(0,),
    )


def back_input(gate_back, up_back, gate_mat, up_mat, dots):
    rows, ff = gate_back.shape
    width = gate_mat.shape[0]
    block = rows // SIDE
    wide = width + dots.shape[1]

    def kernel(gb, ub, wg, wu, dots, o0, o1, o2, o3, o4, whole, sems):
        whole[:, width:] = dots[...]
        for n in range(0, width, TILE):
            at = slice(n, n + TILE)
            val = lax.dot_general(gb[...], wg[at, :], NT, preferred_element_type=F32)
            val += lax.dot_general(ub[...], wu[at, :], NT, preferred_element_type=F32)
            whole[:, at] = val.astype(BF)
        stores, row = [], 0
        for i, o in enumerate((o0, o1, o2, o3, o4)):
            stores.append(pltpu.make_async_copy(whole.at[pl.ds(row, o.shape[0]), :], o, sems.at[i]))
            row += o.shape[0]
        for c in stores:
            c.start()
        for c in stores:
            c.wait()

    return call(
        kernel,
        [shape((r, wide)) for r in part_rows(block)],
        [gate_back, up_back, gate_mat, up_mat, dots],
        [pltpu.VMEM((rows, wide), BF), SEMS],
        hidden_out=range(PARTS),
    )


def gate_up_terms(whole, gate_back, up_back, shares, after):
    width = whole.shape[1]
    ff = gate_back.shape[1]
    part = width // shares

    def kernel(x, gb, ub, out, mark):
        mark[...] = jnp.zeros(mark.shape, F32)
        row = 0
        for ref in (gb, ub):
            for n in range(0, ff, TILE):
                value = lax.dot_general(x[...], ref[:, n : n + TILE], TN, preferred_element_type=F32)
                value = value.astype(BF)
                for s in range(shares):
                    out[s, row : row + part, :] = value[s * part : (s + 1) * part, :]
                row += part

    return call(
        kernel,
        [shape((shares, 2 * (ff // TILE) * part, TILE)), shape((8, 128), F32)],
        [whole, gate_back, up_back],
        after=after,
    )


def down_terms(hidden, whole, order, shares, after):
    ff, width = hidden.shape[1], whole.shape[1]
    part = width // shares
    half = shares // 2

    def kernel(order, hid, x, give, keep):
        for k in range(shares):
            cols = pl.ds(pl.multiple_of(order[k] * part, part), part)
            out = give if k < half else keep
            out[k % half] = lax.dot_general(hid[...], x[:, cols], TN, preferred_element_type=F32).astype(BF)

    return call(kernel, [shape((half, ff, part))] * 2, [hidden, whole], scalars=[order], after=after)


def merge_rows(placer, blocks, after):
    group, rows = placer.shape
    width = blocks[0].shape[1]
    rows_dev = group // SIDE

    def kernel(x0, x1, x2, x3, x4, place, o0, o1, o2, o3, o4, whole, sems):
        stack_blocks((x0, x1, x2, x3, x4), whole, sems)
        for at in range(0, width, TILE):
            cols = slice(at, min(at + TILE, width))
            val = jnp.dot(place[...], whole[:, cols], preferred_element_type=F32).astype(BF)
            for o, v in zip((o0, o1, o2, o3, o4), split_rows(val, rows_dev)):
                o[:, cols] = v

    return call(
        kernel,
        [shape((r, width)) for r in part_rows(rows_dev)],
        [placer],
        [pltpu.VMEM((rows, width), BF), SEMS],
        blocks=blocks,
        after=after,
    )


def add_halves(keep, got, after):
    def kernel(a, b, *outs):
        for k, o in enumerate(outs):
            o[...] = (a[k].astype(F32) + b[k].astype(F32)).astype(BF)

    return call(kernel, [shape(keep.shape[1:])] * keep.shape[0], [keep, got], after=after)


def add_all(terms):
    def kernel(*refs):
        refs[-1][...] = sum(r[...].astype(F32) for r in refs[:-1]).astype(BF)

    return call(kernel, [shape(terms[0].shape)], terms)[0]


def finish(terms, expert_ids, gate_probs, experts):
    rows, fanout = expert_ids.shape
    width = terms[0].shape[1] - 128
    far = part_rows(rows)[2]

    def kernel(experts, x0, x1, x2, x3, x4, ids, probs, grad, prob):
        for at in (slice(0, far), slice(far, rows)):
            parts = (x0[at, :], x1[at, :], (x2 if at.start == 0 else x3)[...], x4[at, :])
            grad[at, :] = sum(p[:, :width].astype(F32) for p in parts).astype(BF)
            total = jnp.zeros((at.stop - at.start, fanout), F32)
            for s in range(SIDE):
                vals = parts[s][:, width:].astype(F32)
                for d in range(SIDE):
                    total += jnp.where(ids[at, :] == experts[s * SIDE + d], vals[:, d : d + 1], 0.0)
            prob[at, :] = (total / probs[at, :].astype(F32)).astype(BF)

    return call(
        kernel,
        [shape((rows, width)), shape((rows, fanout))],
        [*terms, expert_ids, gate_probs],
        scalars=[experts],
        cost=0.000108,
    )


def body(tokens, expert_ids, gate_probs, out_grad, w_gate, w_up, w_down):
    rows_dev, width = tokens.shape
    fanout = expert_ids.shape[1]
    n_dp = lax.axis_size("dp")
    groups = lax.axis_size("expert")
    mean_load = rows_dev * fanout // groups
    capacity = min(rows_dev, mean_load + max(2, rows_dev * fanout // (16 * groups)))
    block = SIDE * capacity

    dp_at = lax.axis_index("dp")
    x_at, z_at = coords(lax.axis_index("expert"))
    even = dp_at % 2 == 0
    a_at = jnp.where(even, x_at, z_at)
    b_at = jnp.where(even, z_at, x_at)

    def expert_of(a, b):
        a, b = a % SIDE, b % SIDE
        return jnp.where(even, a * SIDE + b, b * SIDE + a)

    def along(v, step, core):
        if step % SIDE == 0:
            return v
        return permuted(
            v, n_dp, lambda y, c, x, z: (y, c, x + step, z) if c == core else (y, c, x, z + step)
        )

    first = lambda v, step: along(v, step, 0)
    second = lambda v, step: along(v, step, 1)

    experts = jnp.stack([expert_of(a_at + s, b_at + d) for s in range(SIDE) for d in range(SIDE)])
    near = (dp_at // 2 + jnp.arange(SIDE, dtype=jnp.int32)) % SIDE * 2
    order = jnp.concatenate([near + 1 - dp_at % 2, near + dp_at % 2])
    packed, experts, order = pack(tokens, expert_ids, gate_probs, experts.astype(jnp.int32), order)
    tok_sources = [first(packed, s) for s in range(SIDE)]
    grad_sources = [first(out_grad, s) for s in range(SIDE)]

    def exchange(send, parts, step):
        own, near, far_a, far_b, back = parts
        return [
            own,
            send(near, step),
            send(send(far_a, step), step),
            send(send(far_b, -step), -step),
            send(back, -step),
        ]

    *picked, slot, weight = pick_tokens(tok_sources, experts, width, fanout, block)
    rows_in = exchange(second, picked, 1)
    route_grad = exchange(second, pick_grads(grad_sources, slot, weight, block), 1)

    gate_mat, up_mat, down_mat = w_gate[0], w_up[0], w_down[0]
    ff = gate_mat.shape[1]
    own, near, far_a, far_b, back = rows_in
    early = forward([own, near, back], [0, block, 3 * block], gate_mat, up_mat)
    late_rows = [2 * block, 2 * block + far_a.shape[0]]
    rows_all, hidden, gate_k, up_k = forward([far_a, far_b], late_rows, gate_mat, up_mat, early)
    placer = place_matrix(slot, block)
    grad_all, gate_back, up_back, dots = back_hidden(route_grad, down_mat, gate_k, up_k, hidden)

    parts = back_input(gate_back, up_back, gate_mat, up_mat, dots)
    terms, mark = gate_up_terms(rows_all, gate_back, up_back, n_dp, [parts[0]])
    owned = lax.psum_scatter(terms, "dp", scatter_dimension=0, tiled=True)[0]
    merged = merge_rows(placer, exchange(second, parts, -1), [mark])
    give, keep = down_terms(hidden, grad_all, order, n_dp, [merged[0]])
    got = permuted(give, n_dp, lambda y, c, x, z: (y, 1 - c, x, z))
    ends = exchange(first, merged, -1)
    sums = add_halves(keep, got, [])
    far = [permuted(sums[k], n_dp, lambda y, c, x, z: (y + k, c, x, z)) for k in range(1, SIDE)]
    down_own = add_all([sums[0], *far])
    token_grad, prob_grad = finish(ends, expert_ids, gate_probs, experts)

    share = width // n_dp

    def tile_cols(at):
        return jnp.concatenate([owned[at + t * share : at + (t + 1) * share] for t in range(ff // TILE)], axis=1)

    half = ff // TILE * share
    return (token_grad, prob_grad, tile_cols(0)[None], tile_cols(half)[None], down_own[None])


def solution(mesh):
    rows = P(("dp", "expert"), None)
    mats = P("expert", None, None)
    return jax.shard_map(
        body,
        mesh=mesh,
        in_specs=(rows, rows, rows, rows, mats, mats, mats),
        out_specs=(rows, rows, P("expert", "dp", None), P("expert", "dp", None), P("expert", None, "dp")),
        check_vma=False,
    )
```

```python
import jax
import jax.numpy as jnp
from jax import lax
from jax.experimental import pallas as pl
from jax.experimental.pallas import tpu as pltpu
from jax.sharding import PartitionSpec as P

AXES = ("dp", "expert")
SIDE = 4
BF = jnp.bfloat16
F32 = jnp.float32
TILE = 256
VMEM_LIMIT = 16 * 2**20

NT = (((1,), (1,)), ((), ()))
TN = (((0,), (0,)), ((), ()))


def coords(expert):
    return expert // SIDE, expert % SIDE


def permuted(value, n_dp, target):
    pairs = []
    for dp in range(n_dp):
        for e in range(SIDE * SIDE):
            y, c, x, z = target(dp // 2, dp % 2, *coords(e))
            to = (y % SIDE * 2 + c) * SIDE * SIDE + x % SIDE * SIDE + z % SIDE
            pairs.append((dp * SIDE * SIDE + e, to))
    return lax.ppermute(value, AXES, pairs)


def call(kernel, out_shape, args, scratch=(), scalars=(), blocks=(), after=(), scalars_out=0, hidden_out=(), cost=0.0):
    vmem = pl.BlockSpec(memory_space=pltpu.VMEM)
    smem = pl.BlockSpec(memory_space=pltpu.SMEM)
    anywhere = pl.BlockSpec(memory_space=pl.ANY)

    def run(*refs):
        kernel(*refs[len(after) :])

    return pl.pallas_call(
        run,
        in_specs=[anywhere] * len(after)
        + [smem] * len(scalars)
        + [anywhere] * len(blocks)
        + [vmem] * len(args),
        out_specs=[
            anywhere if i in hidden_out else vmem if i < len(out_shape) - scalars_out else smem
            for i in range(len(out_shape))
        ],
        out_shape=list(out_shape),
        scratch_shapes=list(scratch),
        compiler_params=pltpu.CompilerParams(vmem_limit_bytes=VMEM_LIMIT),
        cost_estimate=pl.CostEstimate(
            flops=1000 + int(cost * 1e15), bytes_accessed=1000 + int(cost * 3.5e12), transcendentals=0
        ),
    )(*after, *scalars, *blocks, *args)


def shape(dims, kind=BF):
    return jax.ShapeDtypeStruct(dims, kind)


def stack_blocks(blocks, whole, sems):
    copies, row = [], 0
    for i, b in enumerate(blocks):
        rows = b.shape[0]
        copies.append(pltpu.make_async_copy(b, whole.at[pl.ds(row, rows), :], sems.at[i]))
        row += rows
    for c in copies:
        c.start()
    for c in copies:
        c.wait()


SEMS = pltpu.SemaphoreType.DMA((SIDE,))


def pack(tokens, expert_ids, gate_probs, experts, order):
    rows, width = tokens.shape
    fanout = expert_ids.shape[1]

    def kernel(experts, order, tok, ids, probs, out, experts_out, order_out):
        for i in range(experts.shape[0]):
            experts_out[i] = experts[i]
        for i in range(order.shape[0]):
            order_out[i] = order[i]
        out[:, :width] = tok[...]
        out[:, width:] = jnp.concatenate(
            [
                ids[...].astype(F32),
                probs[...].astype(F32),
                jnp.zeros((rows, 128 - 2 * fanout), F32),
            ],
            axis=1,
        ).astype(BF)

    return call(
        kernel,
        [shape((rows, width + 128)), shape(experts.shape, jnp.int32), shape(order.shape, jnp.int32)],
        [tokens, expert_ids, gate_probs],
        scalars=[experts, order],
        scalars_out=2,
    )


def onehot_dots(onehot, whole, outs):
    width = outs[0].shape[1]
    for d, o in enumerate(outs):
        hot = onehot(d)
        for at in range(0, width, 512):
            cols = slice(at, at + 512)
            o[:, cols] = jnp.dot(hot, whole[:, cols], preferred_element_type=F32).astype(BF)


def pick_tokens(sources, dests, width, fanout, block):
    rows_dev = sources[0].shape[0]
    group = SIDE * rows_dev

    def kernel(dest, x0, x1, x2, x3, o0, o1, o2, o3, slot, weight, whole, sems):
        stack_blocks((x0, x1, x2, x3), whole, sems)
        hits, probs = [], []
        sheets = [
            jnp.transpose(whole[s * rows_dev : (s + 1) * rows_dev, width:].astype(F32)) for s in range(SIDE)
        ]
        for d in range(SIDE):
            hit, prob = [], []
            for m in sheets:
                same = jnp.where(m[:fanout, :] == dest[d].astype(F32), 1.0, 0.0)
                hit.append(jnp.sum(same, axis=0, keepdims=True))
                prob.append(jnp.sum(same * m[fanout : 2 * fanout, :], axis=0, keepdims=True))
            hits.append(jnp.concatenate(hit, axis=1))
            probs.append(jnp.concatenate(prob, axis=1))
        hits = jnp.concatenate(hits + [jnp.zeros((SIDE, group), F32)], axis=0)
        probs = jnp.concatenate(probs + [jnp.zeros((SIDE, group), F32)], axis=0)
        earlier = lax.broadcasted_iota(jnp.int32, (group, group), 0) < lax.broadcasted_iota(
            jnp.int32, (group, group), 1
        )
        rank = jnp.dot(
            hits.astype(BF), jnp.where(earlier, 1.0, 0.0).astype(BF), preferred_element_type=F32
        )
        slot[...] = jnp.where(hits > 0.5, rank, -4096.0)
        weight[...] = probs
        row = lax.broadcasted_iota(jnp.int32, (block, group), 0).astype(F32)
        onehot_dots(
            lambda d: jnp.where(row == slot[d : d + 1, :], 1.0, 0.0).astype(BF),
            whole,
            (o0, o1, o2, o3),
        )

    return call(
        kernel,
        [shape((r, width)) for r in [block] * SIDE] + [shape((2 * SIDE, group), F32)] * 2,
        [],
        [pltpu.VMEM((group, width + 128), BF), SEMS],
        [dests],
        sources,
    )


def pick_grads(sources, slot, weight, block):
    rows_dev, width = sources[0].shape
    group = SIDE * rows_dev

    def kernel(x0, x1, x2, x3, slot, weight, o0, o1, o2, o3, whole, sems):
        stack_blocks((x0, x1, x2, x3), whole, sems)
        row = lax.broadcasted_iota(jnp.int32, (block, group), 0).astype(F32)
        onehot_dots(
            lambda d: jnp.where(row == slot[d : d + 1, :], weight[d : d + 1, :], 0.0).astype(BF),
            whole,
            (o0, o1, o2, o3),
        )

    return call(
        kernel,
        [shape((r, width)) for r in [block] * SIDE],
        [slot, weight],
        [pltpu.VMEM((group, width), BF), SEMS],
        blocks=sources,
    )


def place_matrix(slot, block):
    group = slot.shape[1]

    def kernel(slot, place):
        tall = jnp.transpose(jnp.concatenate([slot[...]] * 16, axis=0))
        lane = lax.broadcasted_iota(jnp.int32, (group, SIDE * block), 1).astype(F32)
        back = jnp.zeros((group, SIDE * block), F32)
        for d in range(SIDE):
            back = jnp.where(lane == tall[:, d : d + 1] + float(d * block), 1.0, back)
        place[...] = back.astype(BF)

    return call(kernel, [shape((group, SIDE * block))], [slot])[0]


def forward(blocks, gate_mat, up_mat):
    width = blocks[0].shape[1]
    ff = gate_mat.shape[1]
    rows = sum(b.shape[0] for b in blocks)
    half = rows // 2

    def kernel(x0, x1, x2, x3, wg, wu, whole, hidden, gate_k, up_k, sems):
        stack_blocks((x0, x1, x2, x3), whole, sems)
        for n in range(0, ff, TILE):
            cols = slice(n, n + TILE)
            for h in (0, half):
                at = slice(h, h + half)
                g = jnp.dot(whole[at, :], wg[:, cols], preferred_element_type=F32)
                u = jnp.dot(whole[at, :], wu[:, cols], preferred_element_type=F32)
                s = jax.nn.sigmoid(g)
                act = g * s
                hidden[at, cols] = (act * u).astype(BF)
                gate_k[at, cols] = (u * s * (1.0 + g * (1.0 - s))).astype(BF)
                up_k[at, cols] = act.astype(BF)

    return call(
        kernel,
        [shape((rows, width))] + [shape((rows, ff))] * 3,
        [gate_mat, up_mat],
        [SEMS],
        blocks=blocks,
    )


def back_hidden(blocks, down_mat, gate_k, up_k, hidden):
    block, width = blocks[0].shape
    ff = down_mat.shape[0]
    rows = sum(b.shape[0] for b in blocks)
    half = rows // 2

    def kernel(x0, x1, x2, x3, wd, gk, uk, hid, out, gate_back, up_back, dots, whole, total, sems):
        stack_blocks((x0, x1, x2, x3), whole, sems)
        store = pltpu.make_async_copy(whole, out, sems.at[0])
        store.start()
        for n in range(0, ff, TILE):
            cols = slice(n, n + TILE)
            for h in (0, half):
                at = slice(h, h + half)
                hg = lax.dot_general(whole[at, :], wd[cols, :], NT, preferred_element_type=F32)
                gate_back[at, cols] = (hg * gk[at, cols].astype(F32)).astype(BF)
                up_back[at, cols] = (hg * uk[at, cols].astype(F32)).astype(BF)
                term = hg * hid[at, cols].astype(F32)
                term = term[:, :128] + term[:, 128:]
                total[at, :] = term if n == 0 else total[at, :] + term
        for d in range(SIDE):
            at = slice(d * block, (d + 1) * block)
            lane = lax.broadcasted_iota(jnp.int32, (block, 128), 1)
            dot = jnp.sum(total[at, :], axis=1, keepdims=True)
            dots[at, :] = jnp.where(lane == d, dot, 0.0).astype(BF)
        store.wait()

    return call(
        kernel,
        [shape((rows, width)), shape((rows, ff)), shape((rows, ff)), shape((rows, 128))],
        [down_mat, gate_k, up_k, hidden],
        [pltpu.VMEM((rows, width), BF), pltpu.VMEM((rows, 128), F32), SEMS],
        blocks=blocks,
        hidden_out=(0,),
    )


def back_input(gate_back, up_back, gate_mat, up_mat, dots):
    rows, ff = gate_back.shape
    width = gate_mat.shape[0]
    block = rows // SIDE
    wide = width + dots.shape[1]

    def kernel(gb, ub, wg, wu, dots, o0, o1, o2, o3, whole, sems):
        whole[:, width:] = dots[...]
        for n in range(0, width, TILE):
            at = slice(n, n + TILE)
            val = lax.dot_general(gb[...], wg[at, :], NT, preferred_element_type=F32)
            val += lax.dot_general(ub[...], wu[at, :], NT, preferred_element_type=F32)
            whole[:, at] = val.astype(BF)
        stores, row = [], 0
        for i, o in enumerate((o0, o1, o2, o3)):
            stores.append(pltpu.make_async_copy(whole.at[pl.ds(row, o.shape[0]), :], o, sems.at[i]))
            row += o.shape[0]
        for c in stores:
            c.start()
        for c in stores:
            c.wait()

    return call(
        kernel,
        [shape((r, wide)) for r in [block] * SIDE],
        [gate_back, up_back, gate_mat, up_mat, dots],
        [pltpu.VMEM((rows, wide), BF), SEMS],
        hidden_out=range(SIDE),
    )


def gate_up_terms(whole, gate_back, up_back, shares, after):
    width = whole.shape[1]
    ff = gate_back.shape[1]
    part = width // shares

    def kernel(x, gb, ub, out, mark):
        mark[...] = jnp.zeros(mark.shape, F32)
        row = 0
        for ref in (gb, ub):
            for n in range(0, ff, TILE):
                value = lax.dot_general(x[...], ref[:, n : n + TILE], TN, preferred_element_type=F32)
                value = value.astype(BF)
                for s in range(shares):
                    out[s, row : row + part, :] = value[s * part : (s + 1) * part, :]
                row += part

    return call(
        kernel,
        [shape((shares, 2 * (ff // TILE) * part, TILE)), shape((8, 128), F32)],
        [whole, gate_back, up_back],
        after=after,
    )


def down_terms(hidden, whole, order, shares, after):
    ff, width = hidden.shape[1], whole.shape[1]
    part = width // shares
    half = shares // 2

    def kernel(order, hid, x, give, keep):
        for k in range(shares):
            cols = pl.ds(pl.multiple_of(order[k] * part, part), part)
            out = give if k < half else keep
            out[k % half] = lax.dot_general(hid[...], x[:, cols], TN, preferred_element_type=F32).astype(BF)

    return call(kernel, [shape((half, ff, part))] * 2, [hidden, whole], scalars=[order], after=after)


def merge_rows(placer, blocks, after):
    group, rows = placer.shape
    width = blocks[0].shape[1]
    rows_dev = group // SIDE

    def kernel(x0, x1, x2, x3, place, o0, o1, o2, o3, whole, sems):
        stack_blocks((x0, x1, x2, x3), whole, sems)
        for at in range(0, width, TILE):
            cols = slice(at, min(at + TILE, width))
            val = jnp.dot(place[...], whole[:, cols], preferred_element_type=F32).astype(BF)
            for s, o in enumerate((o0, o1, o2, o3)):
                o[:, cols] = val[s * rows_dev : (s + 1) * rows_dev, :]

    return call(
        kernel,
        [shape((r, width)) for r in [rows_dev] * SIDE],
        [placer],
        [pltpu.VMEM((rows, width), BF), SEMS],
        blocks=blocks,
        after=after,
    )


def add_halves(keep, got, after):
    def kernel(a, b, *outs):
        for k, o in enumerate(outs):
            o[...] = (a[k].astype(F32) + b[k].astype(F32)).astype(BF)

    return call(kernel, [shape(keep.shape[1:])] * keep.shape[0], [keep, got], after=after)


def add_all(terms):
    def kernel(*refs):
        refs[-1][...] = sum(r[...].astype(F32) for r in refs[:-1]).astype(BF)

    return call(kernel, [shape(terms[0].shape)], terms)[0]


def finish(terms, expert_ids, gate_probs, experts):
    rows, fanout = expert_ids.shape
    width = terms[0].shape[1] - 128

    def kernel(experts, x0, x1, x2, x3, ids, probs, grad, prob):
        parts = (x0, x1, x2, x3)
        grad[...] = sum(p[:, :width].astype(F32) for p in parts).astype(BF)
        total = jnp.zeros((rows, fanout), F32)
        for s in range(SIDE):
            vals = parts[s][:, width:].astype(F32)
            for d in range(SIDE):
                total += jnp.where(ids[...] == experts[s * SIDE + d], vals[:, d : d + 1], 0.0)
        prob[...] = (total / probs[...].astype(F32)).astype(BF)

    return call(
        kernel,
        [shape((rows, width)), shape((rows, fanout))],
        [*terms, expert_ids, gate_probs],
        scalars=[experts],
        cost=0.000117,
    )


def body(tokens, expert_ids, gate_probs, out_grad, w_gate, w_up, w_down):
    rows_dev, width = tokens.shape
    fanout = expert_ids.shape[1]
    n_dp = lax.axis_size("dp")
    groups = lax.axis_size("expert")
    mean_load = rows_dev * fanout // groups
    capacity = min(rows_dev, mean_load + max(2, rows_dev * fanout // (16 * groups)))
    block = SIDE * capacity

    dp_at = lax.axis_index("dp")
    x_at, z_at = coords(lax.axis_index("expert"))
    even = dp_at % 2 == 0
    a_at = jnp.where(even, x_at, z_at)
    b_at = jnp.where(even, z_at, x_at)

    def expert_of(a, b):
        a, b = a % SIDE, b % SIDE
        return jnp.where(even, a * SIDE + b, b * SIDE + a)

    def along(v, step, core):
        if step % SIDE == 0:
            return v
        return permuted(
            v, n_dp, lambda y, c, x, z: (y, c, x + step, z) if c == core else (y, c, x, z + step)
        )

    first = lambda v, step: along(v, step, 0)
    second = lambda v, step: along(v, step, 1)

    experts = jnp.stack([expert_of(a_at + s, b_at + d) for s in range(SIDE) for d in range(SIDE)])
    near = (dp_at // 2 + jnp.arange(SIDE, dtype=jnp.int32)) % SIDE * 2
    order = jnp.concatenate([near + 1 - dp_at % 2, near + dp_at % 2])
    packed, experts, order = pack(tokens, expert_ids, gate_probs, experts.astype(jnp.int32), order)
    tok_sources = [first(packed, s) for s in range(SIDE)]
    grad_sources = [first(out_grad, s) for s in range(SIDE)]

    def exchange(send, parts, step):
        return [send(v, d * step) for d, v in enumerate(parts)]

    *picked, slot, weight = pick_tokens(tok_sources, experts, width, fanout, block)
    rows_in = exchange(second, picked, 1)
    route_grad = exchange(second, pick_grads(grad_sources, slot, weight, block), 1)

    gate_mat, up_mat, down_mat = w_gate[0], w_up[0], w_down[0]
    ff = gate_mat.shape[1]
    rows_all, hidden, gate_k, up_k = forward(rows_in, gate_mat, up_mat)
    placer = place_matrix(slot, block)
    grad_all, gate_back, up_back, dots = back_hidden(route_grad, down_mat, gate_k, up_k, hidden)

    parts = back_input(gate_back, up_back, gate_mat, up_mat, dots)
    terms, mark = gate_up_terms(rows_all, gate_back, up_back, n_dp, [parts[0]])
    owned = lax.psum_scatter(terms, "dp", scatter_dimension=0, tiled=True)[0]
    give, keep = down_terms(hidden, grad_all, order, n_dp, [mark])
    got = permuted(give, n_dp, lambda y, c, x, z: (y, 1 - c, x, z))
    merged = merge_rows(placer, exchange(second, parts, -1), [mark])
    ends = exchange(first, merged, -1)
    sums = add_halves(keep, got, [merged[0]])
    far = [permuted(sums[k], n_dp, lambda y, c, x, z: (y + k, c, x, z)) for k in range(1, SIDE)]
    down_own = add_all([sums[0], *far])
    token_grad, prob_grad = finish(ends, expert_ids, gate_probs, experts)

    share = width // n_dp

    def tile_cols(at):
        return jnp.concatenate([owned[at + t * share : at + (t + 1) * share] for t in range(ff // TILE)], axis=1)

    half = ff // TILE * share
    return (token_grad, prob_grad, tile_cols(0)[None], tile_cols(half)[None], down_own[None])


def solution(mesh):
    rows = P(("dp", "expert"), None)
    mats = P("expert", None, None)
    return jax.shard_map(
        body,
        mesh=mesh,
        in_specs=(rows, rows, rows, rows, mats, mats, mats),
        out_specs=(rows, rows, P("expert", "dp", None), P("expert", "dp", None), P("expert", None, "dp")),
        check_vma=False,
    )
```
